128 devices in a mesh: expert: 32 (over x, y, core), wshard: 4 (over z).
Axes of the slice: x: 4, y: 4, z: 4, core: 2. Of those that a mesh axis runs over, the one named last changes fastest.
Arguments:
- tokens: bfloat16 [24576, 1024], P(('expert', 'wshard')), may hold values from -6 to 6
- w_query: bfloat16 [1024, 1024], P('wshard'), may hold values from -0.75 to 0.75
- w_key: bfloat16 [1024, 512], P('wshard'), may hold values from -0.75 to 0.75
- w_value: bfloat16 [1024, 512], P('wshard'), may hold values from -0.1875 to 0.1875
- w_out: bfloat16 [1024, 1024], P('wshard'), may hold values from -6 to 6
- w_router: bfloat16 [1024, 32], P('wshard'), may hold values from -0.09375 to 0.09375
- gain_attn: bfloat16 [1024], P('wshard'), may hold values from 0.25 to 1.75
- gain_moe: bfloat16 [1024], P('wshard'), may hold values from 0.25 to 1.75
- w_gate: bfloat16 [32, 1024, 512], P('expert'), may hold values from -0.1875 to 0.1875
- w_up: bfloat16 [32, 1024, 512], P('expert'), may hold values from -0.1875 to 0.1875
- w_down: bfloat16 [32, 512, 1024], P('expert'), may hold values from -6 to 6
- routes: int32 [24576, 8], P(('expert', 'wshard')), may hold values from 0 to 31, all different within a row; in each aligned block of 192 rows (0 to 191, 192 to 383, ...) at most 64 rows name the same one
- seq_split: int32 [32], P('expert'), may hold values from 672 to 768, as said below
- cotangent: bfloat16 [24576, 1024], P(('expert', 'wshard')), may hold values from -6 to 6
Outputs:
- output: float32 [24576, 1024], P(('expert', 'wshard'))
- input_grad: float32 [24576, 1024], P(('expert', 'wshard'))
- grad_query: float32 [1024, 1024], P('wshard')
- grad_key: float32 [1024, 512], P('wshard')
- grad_value: float32 [1024, 512], P('wshard')
- grad_out: float32 [1024, 1024], P('wshard')
- grad_router: float32 [1024, 32], P('wshard')
- grad_gain_attn: float32 [1024], P('wshard')
- grad_gain_moe: float32 [1024], P('wshard')
- grad_gate: float32 [32, 1024, 512], P('expert', 'wshard')
- grad_up: float32 [32, 1024, 512], P('expert', 'wshard')
- grad_down: float32 [32, 512, 1024], P('expert', 'wshard')
The draws below stay inside these ranges and needn't reach their ends.
Inputs may be any that keep to these rules, and one draw needn't show every extreme that they name: `routes`: each row names 8 different experts. Among the 192 rows of one device no expert is named by more than 64 rows, a bound that some block reaches; every expert is named by some row. The first seq_split rows of a group form one sequence and the rest a second one, empty where seq_split is 768; both ends of the range occur in every draw.
All inputs are finite; a program needn't handle non-finite values.
Results may differ from the reference program's by a relative error of at most 0.025.
Values may be sent and summed in bfloat16 or wider, within the bound.
No kernel may reach another device: no remote copies, remote signals or barrier semaphores. Data moves between devices by JAX's collectives and lax.ppermute only.
A program may use at most 192 MiB of HBM per device.

```python
import math
import jax
import jax.numpy as jnp
import numpy as np
from jax import lax

D = 1024
HEADS = 16
KV_HEADS = 8
HEAD_DIM = 64
FF = 512
TOP = 8
TOK_DEV = 192
EXPERTS = 32
CAP = 64
GROUP_TOK = 768
GROUPS = 32
TOKENS = 24576
N_EXPERT = 32
N_WSHARD = 4


def draw_seq_split(key, part):
    key = jax.random.fold_in(key, 11)
    short_key, pick_key, other_key = jax.random.split(key, 3)
    remainder = jax.random.randint(short_key, (GROUPS,), 0, TOK_DEV // 2 + 1)
    chosen = jax.random.randint(pick_key, (), 0, GROUPS)
    other = (chosen + 1 + jax.random.randint(other_key, (), 0, GROUPS - 1)) % GROUPS
    places = jnp.arange(GROUPS, dtype=jnp.int32)
    remainder = jnp.where(places == chosen, 0, remainder)
    remainder = jnp.where(places == other, TOK_DEV // 2, remainder)
    return (GROUP_TOK - remainder).astype(jnp.int32)


def block_scale(rng, shape, cuts, smallest, top_value):
    gain = 1.0
    for axis_at, shards_of in cuts:
        heights = jax.random.uniform(jax.random.fold_in(jax.random.fold_in(rng, 6), axis_at), (shards_of,), jnp.float32, smallest / len(cuts), top_value / len(cuts))
        gain = gain * jnp.repeat(jnp.exp(heights), shape[axis_at] // shards_of).reshape((-1,) + (1,) * (len(shape) - 1 - axis_at))
    return gain


def assign_block(rng, own, number, rows, amount, top, most, slope):
    order = jax.random.permutation(rng, amount)
    heavy_load, common = load_shares(amount, rows * top, most, slope, True), load_shares(amount, rows * top, most, slope, False)
    places = jnp.arange(amount)

    def named(lengths, turn):
        used = int((lengths > 0).sum())
        fixed = max(1, used // 4)
        shifted = fixed + (places - fixed + turn * (used - fixed)) % max(1, amount - fixed)
        return jnp.zeros((amount,), jnp.int32).at[order[jnp.where(places < fixed, places, shifted)]].set(jnp.asarray(lengths, jnp.int32))

    lengths = jnp.where(number % 4 == 0, named(heavy_load, number // 4), named(common, number - number // 4 - 1))
    mixed = jax.random.permutation(jax.random.fold_in(own, 3), amount)
    donor, taker = mixed[0:amount // 2 * 2:2], mixed[1:amount // 2 * 2:2]
    room = jnp.minimum(lengths[donor] - 1, most - lengths[taker]) // 2
    room = jnp.where((donor == order[0]) | (taker == order[0]) | (lengths[taker] == 0), 0, jnp.maximum(room, 0))
    shifted = jax.random.randint(jax.random.fold_in(own, 4), (amount // 2,), 0, 1 << 20) % (room + 1)
    lengths = lengths.at[donor].add(-shifted).at[taker].add(shifted)
    labels = jnp.searchsorted(jnp.cumsum(lengths), jnp.arange(rows * top), side="right").astype(jnp.int32)
    grid = labels.reshape(top, rows).T
    grid = grid[jax.random.permutation(jax.random.fold_in(own, 1), rows)]
    turn = jax.random.randint(jax.random.fold_in(own, 2), (rows, 1), 0, top)
    return jnp.take_along_axis(grid, (jnp.arange(top)[None, :] + turn) % top, axis=1)


def load_shares(amount, total, reach, slope, full):
    loads = [(1 << 20) // math.isqrt(grade ** slope) + 1 for grade in range(1, amount + 1)]
    largest = reach if full else min(reach, max(-(-total // amount), total * loads[0] // sum(loads)))
    least = 1 if total - largest >= amount - 1 else 0
    holding, spare = [largest] + [least] * (amount - 1), total - largest - least * (amount - 1)
    while spare > 0:
        movable = [i for i in range(1, amount) if holding[i] < largest] or [i for i in range(1, amount) if holding[i] < reach]
        pool, remaining = sum([loads[i] for i in movable]), spare
        for i in movable:
            extra = min(reach - holding[i], max(1, remaining * loads[i] // pool), spare)
            holding[i] = holding[i] + extra
            spare = spare - extra
    return np.array(holding)


def gaussian(key, shape, deviation, limit, cuts=(), kind=jnp.bfloat16):
    array = jax.random.normal(key, shape, jnp.float32) * deviation
    if len(cuts) > 0:
        array = block_scale(key, shape, cuts, -0.22, 0.18) * array
    return jnp.clip(array, min=-limit, max=limit).astype(kind)


def setup_inputs(seed: int = 0) -> dict:
    key_list = jax.random.split(jax.random.key(seed), 15)
    tokens = gaussian(key_list[0], (TOKENS, D), 1.0, 6.0, ((0, 128),))
    w_query = gaussian(key_list[1], (D, HEADS * HEAD_DIM), (D // 16) ** -0.5, 0.75, ((0, 4),))
    w_key = gaussian(key_list[2], (D, KV_HEADS * HEAD_DIM), (D // 16) ** -0.5, 0.75, ((0, 4),))
    w_value = gaussian(key_list[3], (D, KV_HEADS * HEAD_DIM), D ** -0.5, 0.1875, ((0, 4),))
    w_out = gaussian(key_list[4], (HEADS * HEAD_DIM, D), 1 ** -0.5, 6.0, ((0, 4),))
    w_router = gaussian(key_list[5], (D, EXPERTS), (4 * D) ** -0.5, 0.09375, ((0, 4),))
    gain_attn = jnp.clip(1.0 + 0.15 * jax.random.normal(key_list[6], (D,), jnp.float32), 0.25, 1.75).astype(jnp.bfloat16)
    gain_moe = jnp.clip(1.0 + 0.15 * jax.random.normal(key_list[7], (D,), jnp.float32), 0.25, 1.75).astype(jnp.bfloat16)
    w_gate = gaussian(key_list[8], (EXPERTS, D, FF), D ** -0.5, 0.1875, ((0, 32),))
    w_up = gaussian(key_list[9], (EXPERTS, D, FF), D ** -0.5, 0.1875, ((0, 32),))
    w_down = gaussian(key_list[10], (EXPERTS, FF, D), 1 ** -0.5, 6.0, ((0, 32),))
    routes_keys = jax.random.split(jax.random.fold_in(key_list[11], 1), TOKENS // TOK_DEV)
    routes_turns = jax.random.permutation(jax.random.fold_in(key_list[11], 3), TOKENS // TOK_DEV)
    routes = jax.vmap(lambda own, number: assign_block(jax.random.fold_in(key_list[11], 2), own, number, TOK_DEV, EXPERTS, TOP, CAP, 1))(routes_keys, routes_turns).reshape((TOKENS, TOP))
    seq_split = draw_seq_split(jax.random.fold_in(key_list[14], 71), 0)
    cotangent = gaussian(key_list[13], (TOKENS, D), 1.0, 6.0, ((0, 128),))
    return dict(tokens=tokens, w_query=w_query, w_key=w_key, w_value=w_value, w_out=w_out, w_router=w_router, gain_attn=gain_attn, gain_moe=gain_moe, w_gate=w_gate, w_up=w_up, w_down=w_down, routes=routes, seq_split=seq_split, cotangent=cotangent)


epsilon = 1e-06
residual_scale = 0.22
score_scale = 0.015625
rope_base = 10000.0
highest = lax.Precision.HIGHEST

@jax.custom_vjp
def low(v):
    return lax.optimization_barrier(v.astype(jnp.bfloat16)).astype(jnp.float32)

@jax.custom_vjp
def low_back(v):
    return v

def low_keep(v):
    return (low(v), None)

def low_pass(kept, grad):
    return (grad,)

def back_keep(v):
    return (v, None)

def back_low(kept, grad):
    return (low(grad),)
low.defvjp(low_keep, low_pass)
low_back.defvjp(back_keep, back_low)

def rms_norm(field, gain_value):
    factor = lax.rsqrt(lax.optimization_barrier(jnp.mean(field * field, axis=-1, keepdims=True)) + epsilon)
    return field * factor * gain_value

def rotate(field, position):
    half_dim = field.shape[-1] // 2
    exponent = jnp.arange(half_dim, dtype=jnp.float32) * (2.0 / field.shape[-1])
    frequency = jnp.power(rope_base, -exponent)
    angles = position[:, None] * frequency[None, :]
    cosine = jnp.cos(angles)[:, None, :]
    sine_part = jnp.sin(angles)[:, None, :]
    front_half = field[..., :half_dim]
    back_half = field[..., half_dim:]
    return jnp.concatenate([front_half * cosine - back_half * sine_part, back_half * cosine + front_half * sine_part], axis=-1)

def group_attention(normed, split_at, w_query, w_key, w_value):
    places = jnp.arange(GROUP_TOK, dtype=jnp.int32)
    in_later = places >= split_at
    position = jnp.where(in_later, places - split_at, places).astype(jnp.float32)
    key_mask = (in_later[:, None] == in_later[None, :]) & (places[None, :] <= places[:, None])
    query_lin = low_back(jnp.dot(normed, w_query, precision=highest)).reshape(GROUP_TOK, HEADS, HEAD_DIM)
    key_lin = low_back(jnp.dot(normed, w_key, precision=highest)).reshape(GROUP_TOK, KV_HEADS, HEAD_DIM)
    queries = low(rotate(query_lin, position))
    key_rows = low(rotate(key_lin, position))
    values = low(low_back(jnp.dot(normed, w_value, precision=highest))).reshape(GROUP_TOK, KV_HEADS, HEAD_DIM)
    grouped = queries.reshape(GROUP_TOK, KV_HEADS, HEADS // KV_HEADS, HEAD_DIM)
    scores = low_back(jnp.einsum('qkgd,tkd->kgqt', grouped, key_rows, precision=highest) * score_scale)
    scores = jnp.where(key_mask[None, None], scores, -1e+30)
    probs = low(jax.nn.softmax(scores, axis=-1))
    mixed_heads = jnp.einsum('kgqt,tkd->qkgd', probs, values, precision=highest)
    return mixed_heads.reshape(GROUP_TOK, HEADS * HEAD_DIM)

def reference(tokens, w_query, w_key, w_value, w_out, w_router, gain_attn, gain_moe, w_gate, w_up, w_down, routes, seq_split, cotangent):
    device_count = N_EXPERT * N_WSHARD
    route_dev = routes.reshape(device_count, TOK_DEV, TOP)
    expert_ids = jnp.arange(EXPERTS, dtype=jnp.int32)
    onehot_int = (route_dev[..., None] == expert_ids).astype(jnp.int32)
    per_token = lax.optimization_barrier(jnp.sum(onehot_int, axis=2))
    before = jnp.cumsum(per_token, axis=1) - per_token
    slot_index = jnp.take_along_axis(before, route_dev, axis=2)
    device_ids = jnp.arange(device_count, dtype=jnp.int32)[:, None, None]
    flat_slot = ((route_dev * device_count + device_ids) * CAP + slot_index).reshape(-1)
    token_ids = jnp.broadcast_to(jnp.arange(TOKENS, dtype=jnp.int32).reshape(device_count, TOK_DEV, 1), route_dev.shape).reshape(-1)
    copy_ids = jnp.arange(TOKENS * TOP, dtype=jnp.int32)
    slot_total = EXPERTS * device_count * CAP
    owners = jnp.zeros((slot_total,), jnp.int32).at[flat_slot].set(token_ids)
    copies = jnp.zeros((slot_total,), jnp.int32).at[flat_slot].set(copy_ids)
    filled = jnp.zeros((slot_total,), jnp.int32).at[flat_slot].set(1)

    def forward(inputs, query_w, key_w, value_w, out_w, router_w, gain_a, gain_m, gate_w, up_w, down_w):
        normed = low(rms_norm(inputs, gain_a))

        def one_group(pieces):
            normed_group, split_at = pieces
            return group_attention(normed_group, split_at, query_w, key_w, value_w)
        mixed_heads = lax.map(jax.checkpoint(one_group), (normed.reshape(GROUPS, GROUP_TOK, D), seq_split))
        mixed_heads = low(low_back(mixed_heads.reshape(TOKENS, HEADS * HEAD_DIM)))
        branch = low_back(jnp.dot(mixed_heads, out_w, precision=highest))
        middle = inputs + residual_scale * branch
        second = low(rms_norm(middle, gain_m))
        logits = jnp.dot(second, router_w, precision=highest)
        gate_probs = jax.nn.softmax(jnp.take_along_axis(logits, routes, axis=1), axis=-1)
        gate_flat = gate_probs.reshape(-1)

        def one_expert(pieces):
            owner_rows, copy_rows, filled_rows, gate_weight, up_weight, down_weight = pieces
            present = filled_rows > 0
            rows_in = low_back(jnp.where(present[:, None], jnp.take(second, owner_rows, axis=0), 0.0))
            gate_lin = low_back(jnp.dot(rows_in, gate_weight, precision=highest))
            up_lin = low_back(jnp.dot(rows_in, up_weight, precision=highest))
            hidden = low(low_back(jax.nn.silu(gate_lin) * up_lin))
            expert_out = low(low_back(jnp.dot(hidden, down_weight, precision=highest)))
            gate_share = jnp.where(present, jnp.take(gate_flat, copy_rows), 0.0)
            return gate_share[:, None] * expert_out
        weighted = lax.map(jax.checkpoint(one_expert), (owners.reshape(EXPERTS, -1), copies.reshape(EXPERTS, -1), filled.reshape(EXPERTS, -1), gate_w, up_w, down_w))
        expert_sum = jax.ops.segment_sum(weighted.reshape(-1, D), owners, num_segments=TOKENS)
        return middle + residual_scale * expert_sum
    primals = (tokens.astype(jnp.float32), w_query.astype(jnp.float32), w_key.astype(jnp.float32), w_value.astype(jnp.float32), w_out.astype(jnp.float32), w_router.astype(jnp.float32), gain_attn.astype(jnp.float32), gain_moe.astype(jnp.float32), w_gate.astype(jnp.float32), w_up.astype(jnp.float32), w_down.astype(jnp.float32))
    output, backward = jax.vjp(forward, *primals)
    grads = backward(cotangent.astype(jnp.float32))
    return (output, grads[0], grads[1], grads[2], grads[3], grads[4], grads[5], grads[6], grads[7], grads[8], grads[9], grads[10])
```

```python
import functools

import jax
import jax.numpy as jnp
from jax import lax
from jax.experimental import pallas as pl
from jax.experimental.pallas import tpu as pltpu
from jax.sharding import PartitionSpec as P

f32 = jnp.float32
bf16 = jnp.bfloat16
epsilon = 1e-06
residual_scale = 0.22
score_scale = 0.015625
rope_base = 10000.0

LANES = 4
OWNERS = 32
ROWS = 192
GROUP = 768
WIDTH = 1024
CAP = 64
SLOTS = OWNERS * CAP
FF = 512
TOP = 8
EXTRA = 128
VMEM = 50 * 1024 * 1024


def nn(a, b):
    return lax.dot_general(a, b, (((1,), (0,)), ((), ())), preferred_element_type=f32)


def nt(a, b):
    return lax.dot_general(a, b, (((1,), (1,)), ((), ())), preferred_element_type=f32)


def tn(a, b):
    return lax.dot_general(a, b, (((0,), (0,)), ((), ())), preferred_element_type=f32)


def iota(shape, axis):
    return lax.broadcasted_iota(jnp.int32, shape, axis)


def split_two(v):
    high = v.astype(bf16)
    return high, (v - high.astype(f32)).astype(bf16)


def call(kernel, name, outs, args, smem=0, scratch=()):
    specs = [pl.BlockSpec(memory_space=pltpu.SMEM)] * smem
    specs += [pl.BlockSpec(memory_space=pltpu.VMEM)] * (len(args) - smem)
    return pl.pallas_call(
        kernel,
        name=name,
        out_shape=[jax.ShapeDtypeStruct(s, d) for s, d in outs],
        in_specs=specs,
        out_specs=[pl.BlockSpec(memory_space=pltpu.VMEM)] * len(outs),
        scratch_shapes=list(scratch),
        compiler_params=pltpu.CompilerParams(vmem_limit_bytes=VMEM),
    )(*args)


def routing_kernel(routes, routes_t, cot, pick, pick_t, mask_out, rows_out):
    lane = iota((ROWS, EXTRA), 1)
    mask = jnp.zeros((ROWS, EXTRA), f32)
    for k in range(TOP):
        mask += (routes[:, k : k + 1] == lane).astype(f32)
    sub = iota((OWNERS, ROWS), 0)
    mask_t = jnp.zeros((OWNERS, ROWS), f32)
    for k in range(TOP):
        mask_t += (routes_t[k : k + 1, :] == sub).astype(f32)
    mask_b = mask.astype(bf16)
    mask_tb = mask_t.astype(bf16)
    i0, i1 = iota((ROWS, ROWS), 0), iota((ROWS, ROWS), 1)
    before = nn((i1 < i0).astype(f32).astype(bf16), mask_b).astype(bf16)
    before_t = nn(mask_tb, (i0 < i1).astype(f32).astype(bf16)).astype(bf16)
    spread = ((iota((EXTRA, SLOTS), 1) // CAP) == iota((EXTRA, SLOTS), 0)).astype(f32).astype(bf16)
    spread_t = ((iota((SLOTS, OWNERS), 0) // CAP) == iota((SLOTS, OWNERS), 1)).astype(f32)
    spread_t = spread_t.astype(bf16)
    slot = (iota((ROWS, SLOTS), 1) % CAP).astype(f32)
    slot_t = (iota((SLOTS, ROWS), 0) % CAP).astype(f32)
    p = jnp.where(nn(before, spread) == slot, nn(mask_b, spread), 0.0)
    p_t = jnp.where(nn(spread_t, before_t) == slot_t, nn(spread_t, mask_tb), 0.0)
    pick[...] = p.astype(bf16)
    pick_t[...] = p_t.astype(bf16)
    mask_out[...] = mask
    p_tb = p_t.astype(bf16)
    rows_out[:, :WIDTH] = nn(p_tb, cot[...]).astype(bf16)
    rows_out[:, WIDTH:] = nn(p_tb, mask_b).astype(bf16)


def swap_halves(t):
    lane = iota(t.shape, 1) % 64
    return jnp.where(lane < 32, pltpu.roll(t, 96, 1), pltpu.roll(t, 32, 1))


def allowed(split, low, rows, keys):
    qi = iota((rows, keys), 0) + low
    kj = iota((rows, keys), 1)
    start = jnp.where(qi >= split, split, 0)
    return (kj <= qi) & (kj >= start)


BLOCK = 256
BLOCKS = GROUP // BLOCK


def head_place(h):
    return h // 2, h % 2, (h // 2) != (h % 2)


def front_kernel(split, x_ref, w_ref, gain, cosine, sine, normed, q_out, k_out, v_out, mixed):
    x = x_ref[...].astype(f32)
    factor = lax.rsqrt(jnp.mean(x * x, axis=-1, keepdims=True) + epsilon)
    normed_b = (x * factor * gain[...]).astype(bf16)
    normed[...] = normed_b
    lin = nn(normed_b, w_ref[:, :512])
    c, s = cosine[...], sine[...]
    for g in range(2):
        part = lin[:, 128 * g : 128 * g + 128]
        q_out[:, 128 * g : 128 * g + 128] = (part * c + swap_halves(part) * s).astype(bf16)
    part = lin[:, 256:384]
    key = part * c + swap_halves(part) * s
    key_b = key.astype(bf16)
    k_out[...] = key_b
    value_b = lin[:, 384:512].astype(bf16)
    v_out[...] = value_b
    keys = (key_b, pltpu.roll(key_b.astype(f32), 64, 1).astype(bf16))
    values = (value_b, pltpu.roll(value_b.astype(f32), 64, 1).astype(bf16))
    low_half = iota((BLOCK, 128), 1) < 64
    for i in range(BLOCKS):
        n = (i + 1) * BLOCK
        ok = allowed(split[0], i * BLOCK, BLOCK, n)
        for g in range(2):
            q2 = q_out[i * BLOCK : (i + 1) * BLOCK, 128 * g : 128 * g + 128].astype(f32) * score_scale
            halves = []
            for half in range(2):
                turned = g != half
                mine = low_half if half == 0 else ~low_half
                qh = jnp.where(mine, q2, 0.0).astype(bf16)
                scores = jnp.where(ok, nt(qh, keys[turned][:n]), -1e30)
                top = jnp.max(scores, axis=-1, keepdims=True)
                e = jnp.exp(scores - top)
                probs = (e / jnp.sum(e, axis=-1, keepdims=True)).astype(bf16)
                halves.append(nn(probs, values[turned][:n]))
            mixed[i * BLOCK : (i + 1) * BLOCK, 128 * g : 128 * g + 128] = jnp.where(
                low_half, halves[0], halves[1]
            ).astype(bf16)


def middle_kernel(mixed, w_out, x_ref, gain, router, mask, pick_t, middle, second, gate, rows_out):
    mid = x_ref[...].astype(f32) + residual_scale * nn(mixed[...], w_out[...])
    middle[...] = mid
    factor = lax.rsqrt(jnp.mean(mid * mid, axis=-1, keepdims=True) + epsilon)
    second_b = (mid * factor * gain[...]).astype(bf16)
    second[...] = second_b
    chosen = mask[...] > 0.5
    logits = jnp.where(chosen, nn(second_b, router[...]), -1e30)
    top = jnp.max(logits, axis=-1, keepdims=True)
    e = jnp.where(chosen, jnp.exp(logits - top), 0.0)
    gate[...] = e / jnp.sum(e, axis=-1, keepdims=True)
    rows_out[...] = nn(pick_t[...], second_b).astype(bf16)


EXPERT_BLOCK = 256


def expert_kernel(
    me, rows, h_up, mask, router, w_gate, w_up, g_rows, hidden, g_gate, g_up, gate_out
):
    r = rows[...]
    lane = iota((EXPERT_BLOCK, EXTRA), 1)
    chosen = mask[...].astype(f32) > 0.5
    logits = jnp.where(chosen, nn(r, router[...]), -1e30)
    top = jnp.max(logits, axis=-1, keepdims=True)
    e = jnp.where(chosen, jnp.exp(logits - top), 0.0)
    total = jnp.sum(e, axis=-1, keepdims=True)
    mine = jnp.sum(jnp.where(lane == me[0], e, 0.0), axis=-1, keepdims=True)
    gate = mine / jnp.where(total > 0, total, 1.0)
    gate_out[...] = jnp.broadcast_to(gate, (EXPERT_BLOCK, EXTRA))
    gate_lin = nn(r, w_gate[...])
    up_lin = nn(r, w_up[...])
    sig = 1.0 / (1.0 + jnp.exp(-gate_lin))
    act = gate_lin * sig
    hidden_b = (act * up_lin).astype(bf16)
    hidden[...] = hidden_b
    up = h_up[...].astype(f32)
    g = residual_scale * jnp.sum(hidden_b.astype(f32) * up, axis=-1, keepdims=True)
    g_hidden = ((residual_scale * gate) * up).astype(bf16).astype(f32)
    gg = (g_hidden * up_lin * (sig * (1.0 + gate_lin * (1.0 - sig)))).astype(bf16)
    gu = (g_hidden * act).astype(bf16)
    g_gate[...] = gg
    g_up[...] = gu
    g_rows[:, :WIDTH] = (nt(gg, w_gate[...]) + nt(gu, w_up[...])).astype(bf16)
    high = g.astype(bf16).astype(f32)
    g_rows[:, WIDTH:] = jnp.where(
        lane == me[0], high, jnp.where(lane == me[0] + OWNERS, g - high, 0.0)
    ).astype(bf16)


def expert_call(me, rows, h_up, ups, router, w_gate, w_up):
    def whole(shape):
        return pl.BlockSpec(shape, lambda i: (0, 0))

    def blocked(width, column=0):
        return pl.BlockSpec((EXPERT_BLOCK, width), lambda i: (i, column))

    return pl.pallas_call(
        expert_kernel,
        name="expert",
        grid=(SLOTS // EXPERT_BLOCK,),
        out_shape=[
            jax.ShapeDtypeStruct((SLOTS, WIDTH + EXTRA), bf16),
            jax.ShapeDtypeStruct((SLOTS, FF), bf16),
            jax.ShapeDtypeStruct((SLOTS, FF), bf16),
            jax.ShapeDtypeStruct((SLOTS, FF), bf16),
            jax.ShapeDtypeStruct((SLOTS, EXTRA), f32),
        ],
        in_specs=[
            pl.BlockSpec(memory_space=pltpu.SMEM),
            blocked(WIDTH),
            blocked(FF),
            blocked(EXTRA, WIDTH // EXTRA),
            whole((WIDTH, EXTRA)),
            whole((WIDTH, FF)),
            whole((WIDTH, FF)),
        ],
        out_specs=[blocked(WIDTH + EXTRA), blocked(FF), blocked(FF), blocked(FF), blocked(EXTRA)],
        compiler_params=pltpu.CompilerParams(vmem_limit_bytes=VMEM),
    )(me, rows, h_up, ups, router, w_gate, w_up)


def return_kernel(
    back, pick, middle, second, gate, cot, router, gain, g_middle_out, g_branch, small_out
):
    ext = nn(pick[...], back[...])
    lane = iota((ROWS, EXTRA), 1)
    tail = ext[:, WIDTH:]
    g_gate = jnp.where(lane < OWNERS, tail + pltpu.roll(tail, EXTRA - OWNERS, 1), 0.0)
    probs = gate[...]
    g_logits = probs * (g_gate - jnp.sum(probs * g_gate, axis=-1, keepdims=True))
    high, low = split_two(g_logits)
    w = router[...]
    g_second = ext[:, :WIDTH] + (nt(high, w) + nt(low, w))
    mid = middle[...]
    factor = lax.rsqrt(jnp.mean(mid * mid, axis=-1, keepdims=True) + epsilon)
    z = mid * factor
    t = g_second * gain[...]
    g_middle = cot[...].astype(f32) + factor * (t - z * jnp.mean(t * z, axis=-1, keepdims=True))
    g_middle_out[...] = g_middle
    g_branch[...] = (residual_scale * g_middle).astype(bf16)
    s = second[...]
    one = (lane == OWNERS).astype(f32).astype(bf16)
    ph, plow = split_two(g_second * z)
    small_out[...] = tn(s, high) + tn(s, low) + tn(ph, one) + tn(plow, one)


def back_kernel(
    split,
    gb,
    gb_cols,
    w_out,
    mixed_all,
    q_ref,
    k_ref,
    v_ref,
    normed,
    x_ref,
    w_ref,
    cosine,
    sine,
    small_in,
    grads,
    g_normed_out,
    g_mixed,
    g_query,
    g_key,
    g_value,
):
    g_mixed[...] = nt(gb[...], w_out[...]).astype(bf16)
    key_b, value_b = k_ref[...], v_ref[...]
    keys = (key_b, pltpu.roll(key_b.astype(f32), 64, 1).astype(bf16))
    values = (value_b, pltpu.roll(value_b.astype(f32), 64, 1).astype(bf16))
    g_key[...] = jnp.zeros_like(g_key)
    g_value[...] = jnp.zeros_like(g_value)
    low_half = iota((BLOCK, 128), 1) < 64
    for i in range(BLOCKS):
        n = (i + 1) * BLOCK
        here = slice(i * BLOCK, (i + 1) * BLOCK)
        ok = allowed(split[0], i * BLOCK, BLOCK, n)
        for g in range(2):
            q2 = q_ref[here, 128 * g : 128 * g + 128].astype(f32) * score_scale
            gm2 = g_mixed[here, 128 * g : 128 * g + 128].astype(f32)
            halves = []
            for half in range(2):
                turned = int(g != half)
                mine = low_half if half == 0 else ~low_half
                qh = jnp.where(mine, q2, 0.0).astype(bf16)
                gm = jnp.where(mine, gm2, 0.0).astype(bf16)
                scores = jnp.where(ok, nt(qh, keys[turned][:n]), -1e30)
                top = jnp.max(scores, axis=-1, keepdims=True)
                e = jnp.exp(scores - top)
                probs = e / jnp.sum(e, axis=-1, keepdims=True)
                gp = nt(gm, values[turned][:n])
                pg = probs * gp
                gs = (pg - probs * jnp.sum(pg, axis=-1, keepdims=True)).astype(bf16)
                halves.append(nn(gs, keys[turned][:n]))
                g_key[turned, :n, :] += tn(gs, qh)
                g_value[turned, :n, :] += tn(probs.astype(bf16), gm)
            g_query[here, 128 * g : 128 * g + 128] = score_scale * jnp.where(
                low_half, halves[0], halves[1]
            )
    c, s = cosine[...], sine[...]

    def unturn(t):
        return (t * c - swap_halves(t) * s).astype(bf16)

    g_lin = jnp.concatenate(
        [
            unturn(g_query[:, :128]),
            unturn(g_query[:, 128:]),
            unturn(g_key[0] + pltpu.roll(g_key[1], 64, 1)),
            (g_value[0] + pltpu.roll(g_value[1], 64, 1)).astype(bf16),
        ],
        axis=1,
    )
    grads[:, :512] = tn(normed[...], g_lin).astype(bf16)
    grads[:, 512:768] = tn(mixed_all[...], gb_cols[...]).astype(bf16)
    g_normed = nt(g_lin, w_ref[:, :512])
    g_normed_out[...] = g_normed.astype(bf16)
    x = x_ref[...].astype(f32)
    y = x * lax.rsqrt(jnp.mean(x * x, axis=-1, keepdims=True) + epsilon)
    one = (iota((GROUP, EXTRA), 1) == OWNERS + 1).astype(f32).astype(bf16)
    ph, plow = split_two(g_normed * y)
    grads[:, 768:] = (small_in[...] + tn(ph, one) + tn(plow, one)).astype(bf16)


def z_shift(value, d):
    return lax.ppermute(value, "wshard", [(i, (i + d) % LANES) for i in range(LANES)])


def by_source(pieces, z, axis=0):
    stacked = jnp.stack(pieces)
    return jnp.concatenate(
        [
            lax.dynamic_index_in_dim(stacked, (z - a) % LANES, 0, keepdims=False)
            for a in range(LANES)
        ],
        axis=axis,
    )


def gather_z(value, z, axis=0):
    return by_source([value] + [z_shift(value, d) for d in (1, 2, 3)], z, axis)


def both_cores(value, core):
    other = lax.ppermute(value, "expert", [(i, i ^ 1) for i in range(OWNERS)])
    first = jnp.where(core == 0, value, other)
    last = jnp.where(core == 0, other, value)
    return first, last


def to_owners(value):
    return lax.all_to_all(value, "expert", 0, 0, tiled=True)


def local(
    tokens,
    w_query,
    w_key,
    w_value,
    w_out,
    w_router,
    gain_attn,
    gain_moe,
    w_gate,
    w_up,
    w_down,
    routes,
    seq_split,
    cotangent,
):
    z = lax.axis_index("wshard")
    me = lax.axis_index("expert")
    core = me % 2
    w_gate, w_up, w_down = w_gate[0], w_up[0], w_down[0]

    pick, pick_t, mask, ups_send = call(
        routing_kernel,
        "routing",
        [
            ((ROWS, SLOTS), bf16),
            ((SLOTS, ROWS), bf16),
            ((ROWS, EXTRA), f32),
            ((SLOTS, WIDTH + EXTRA), bf16),
        ],
        (routes, routes.T, cotangent),
    )
    ups = to_owners(ups_send.reshape(OWNERS, CAP, WIDTH + EXTRA)).reshape(SLOTS, WIDTH + EXTRA)

    x_all = gather_z(tokens, z)
    small = jnp.concatenate(
        [
            w_router,
            gain_attn[:, None],
            gain_moe[:, None],
            jnp.zeros((256, EXTRA - OWNERS - 2), bf16),
        ],
        axis=1,
    )

    def columns_for(dest):
        row = core * 128
        return jnp.concatenate(
            [
                lax.dynamic_slice(w_query, (row, dest * 256), (128, 256)),
                lax.dynamic_slice(w_key, (row, dest * 128), (128, 128)),
                lax.dynamic_slice(w_value, (row, dest * 128), (128, 128)),
                lax.dynamic_slice(small, (row, 0), (128, EXTRA)),
            ],
            axis=1,
        )

    pieces = [columns_for(z)] + [z_shift(columns_for((z + d) % LANES), d) for d in (1, 2, 3)]
    mine = by_source(pieces, z).reshape(LANES, 128, 640)
    first, last = both_cores(mine, core)
    w_all = jnp.stack([first, last], axis=1).reshape(WIDTH, 640)
    small_all = w_all[:, 512:]
    gain_a = small_all[:, OWNERS].astype(f32)[None, :]
    gain_m = small_all[:, OWNERS + 1].astype(f32)[None, :]

    half_out = lax.dynamic_slice(w_out, (core * 128, 0), (128, WIDTH))
    out_mine = gather_z(half_out, z).reshape(LANES, 128, WIDTH)
    first, last = both_cores(out_mine, core)
    out_all = jnp.stack([first, last], axis=1).reshape(WIDTH, WIDTH)

    split_at = seq_split[0]
    places = jnp.arange(GROUP, dtype=jnp.int32)
    position = jnp.where(places >= split_at, places - split_at, places).astype(f32)
    exponent = jnp.arange(32, dtype=f32) * (2.0 / 64)
    angles = position[:, None] * jnp.power(rope_base, -exponent)[None, :]
    cosine, sine = jnp.cos(angles), jnp.sin(angles)
    cosine = jnp.concatenate([cosine] * 4, axis=1)
    sine = jnp.concatenate([-sine, sine] * 2, axis=1)

    normed, query, key, value, mixed = call(
        front_kernel,
        "attention",
        [
            ((GROUP, WIDTH), bf16),
            ((GROUP, 256), bf16),
            ((GROUP, 128), bf16),
            ((GROUP, 128), bf16),
            ((GROUP, 256), bf16),
        ],
        (seq_split, x_all, w_all, gain_a, cosine, sine),
        smem=1,
    )
    by_row = mixed.reshape(LANES, ROWS, 256)

    def rows_for(dest):
        return lax.dynamic_index_in_dim(by_row, dest, 0, keepdims=False)

    mixed_own = by_source(
        [rows_for(z)] + [z_shift(rows_for((z + d) % LANES), d) for d in (1, 2, 3)], z, 1
    )
    middle, second, gate, rows_send = call(
        middle_kernel,
        "middle",
        [
            ((ROWS, WIDTH), f32),
            ((ROWS, WIDTH), bf16),
            ((ROWS, EXTRA), f32),
            ((SLOTS, WIDTH), bf16),
        ],
        (mixed_own, out_all, tokens, gain_m, small_all, mask, pick_t),
    )
    rows_in = to_owners(rows_send.reshape(OWNERS, CAP, WIDTH)).reshape(SLOTS, WIDTH)
    mixed_all = gather_z(mixed, z, 1)

    up_rows = ups[:, :WIDTH]
    h_up = nt(up_rows, w_down).astype(bf16)
    g_rows, hidden, g_gate, g_up, gate_rows = expert_call(
        me.reshape(1), rows_in, h_up, ups, small_all, w_gate, w_up
    )
    back = to_owners(g_rows.reshape(OWNERS, CAP, WIDTH + EXTRA)).reshape(SLOTS, WIDTH + EXTRA)

    row_gate = gate_rows[:, :1]
    expert_out = nn(hidden, w_down).astype(bf16).astype(f32)
    out_back = to_owners((row_gate * expert_out).astype(bf16).reshape(OWNERS, CAP, WIDTH))
    g_out = (residual_scale * row_gate * up_rows.astype(f32)).astype(bf16)
    gate_grad = tn(rows_in, g_gate).astype(bf16)
    up_grad = tn(rows_in, g_up).astype(bf16)
    down_grad = tn(hidden, g_out).astype(bf16)
    packed = jnp.concatenate(
        [
            gate_grad.reshape(LANES, 256, FF),
            up_grad.reshape(LANES, 256, FF),
            down_grad[:, :FF].reshape(LANES, 128, FF),
            down_grad[:, FF:].reshape(LANES, 128, FF),
        ],
        axis=1,
    )

    def part_for(dest):
        return lax.dynamic_index_in_dim(packed, dest, 0, keepdims=False)

    expert_sum = part_for(z).astype(f32)
    for d in (1, 2, 3):
        expert_sum += z_shift(part_for((z + d) % LANES), d).astype(f32)
    gate_share = expert_sum[None, :256]
    up_share = expert_sum[None, 256:512]
    down_share = jnp.concatenate([expert_sum[512:640], expert_sum[640:]], axis=1)[None]

    g_middle, g_branch, small_grad = call(
        return_kernel,
        "return",
        [((ROWS, WIDTH), f32), ((ROWS, WIDTH), bf16), ((WIDTH, EXTRA), f32)],
        (back, pick, middle, second, gate, cotangent, small_all, gain_m),
    )
    branch_all = gather_z(g_branch, z)
    branch_cols = lax.dynamic_slice(branch_all, (0, z * 256), (GROUP, 256))
    grads, g_normed = call(
        back_kernel,
        "attention_back",
        [((WIDTH, 768 + EXTRA), bf16), ((GROUP, WIDTH), bf16)],
        (
            seq_split,
            branch_all,
            branch_cols,
            w_out,
            mixed_all,
            query,
            key,
            value,
            normed,
            x_all,
            w_all,
            cosine,
            sine,
            small_grad,
        ),
        smem=1,
        scratch=[
            pltpu.VMEM((GROUP, 256), bf16),
            pltpu.VMEM((GROUP, 256), f32),
            pltpu.VMEM((2, GROUP, 128), f32),
            pltpu.VMEM((2, GROUP, 128), f32),
        ],
    )

    wide = 768 + EXTRA
    spread = grads.reshape(LANES, OWNERS, 8, wide).transpose(1, 0, 2, 3).reshape(128, 8, wide)
    arrived = lax.all_to_all(spread, ("expert", "wshard"), 0, 0, tiled=True)
    summed = jnp.sum(arrived.reshape(OWNERS, LANES, 8, wide).astype(f32), axis=0)
    small_sum = jnp.sum(summed[:, :, 768:], axis=0)
    strip = jnp.concatenate(
        [summed[a, :, :256] for a in range(LANES)]
        + [summed[a, :, 256:384] for a in range(LANES)]
        + [summed[a, :, 384:512] for a in range(LANES)]
        + [summed[a, :, 512:768] for a in range(LANES)]
        + [small_sum],
        axis=1,
    ).astype(bf16)
    shared = to_owners(jnp.broadcast_to(strip[None], (OWNERS,) + strip.shape))
    shared = shared.reshape(256, strip.shape[1]).astype(f32)

    output = middle + residual_scale * nn(pick, out_back.reshape(SLOTS, WIDTH))

    by_group = g_normed.reshape(LANES, ROWS, WIDTH)

    def normed_for(dest):
        return lax.dynamic_index_in_dim(by_group, dest, 0, keepdims=False)

    g_own = normed_for(z).astype(f32)
    for d in (1, 2, 3):
        g_own += z_shift(normed_for((z + d) % LANES), d).astype(f32)
    x = tokens.astype(f32)
    factor = lax.rsqrt(jnp.mean(x * x, axis=-1, keepdims=True) + epsilon)
    y = x * factor
    t = g_own * gain_a
    input_grad = g_middle + factor * (t - y * jnp.mean(t * y, axis=-1, keepdims=True))

    return (
        output,
        input_grad,
        shared[:, :1024],
        shared[:, 1024:1536],
        shared[:, 1536:2048],
        shared[:, 2048:3072],
        shared[:, 3072 : 3072 + OWNERS],
        shared[:, 3072 + OWNERS + 1],
        shared[:, 3072 + OWNERS],
        gate_share,
        up_share,
        down_share,
    )


def solution(mesh):
    rows = P(("expert", "wshard"), None)
    dense = P("wshard", None)
    expert = P("expert", None, None)
    shard = P("expert", "wshard", None)
    in_specs = (rows,) + (dense,) * 5 + (P("wshard"),) * 2 + (expert,) * 3
    in_specs += (rows, P("expert"), rows)
    out_specs = (rows, rows) + (dense,) * 5 + (P("wshard"),) * 2 + (shard,) * 3
    return jax.shard_map(local, mesh=mesh, in_specs=in_specs, out_specs=out_specs, check_vma=False)
```

```python
import functools

import jax
import jax.numpy as jnp
from jax import lax
from jax.experimental import pallas as pl
from jax.experimental.pallas import tpu as pltpu
from jax.sharding import PartitionSpec as P

f32 = jnp.float32
bf16 = jnp.bfloat16
epsilon = 1e-06
residual_scale = 0.22
score_scale = 0.015625
rope_base = 10000.0

LANES = 4
OWNERS = 32
ROWS = 192
GROUP = 768
WIDTH = 1024
CAP = 64
SLOTS = OWNERS * CAP
FF = 512
TOP = 8
EXTRA = 128
VMEM = 50 * 1024 * 1024


def nn(a, b):
    return lax.dot_general(a, b, (((1,), (0,)), ((), ())), preferred_element_type=f32)


def nt(a, b):
    return lax.dot_general(a, b, (((1,), (1,)), ((), ())), preferred_element_type=f32)


def tn(a, b):
    return lax.dot_general(a, b, (((0,), (0,)), ((), ())), preferred_element_type=f32)


def iota(shape, axis):
    return lax.broadcasted_iota(jnp.int32, shape, axis)


def split_two(v):
    high = v.astype(bf16)
    return high, (v - high.astype(f32)).astype(bf16)


def cost(us):
    return pl.CostEstimate(
        flops=int(us * 1e9), bytes_accessed=int(us * 3.5e6), transcendentals=0
    )


def call(kernel, name, outs, args, us, smem=0, scratch=(), after=()):
    specs = [pl.BlockSpec(memory_space=pltpu.SMEM)] * smem
    specs += [pl.BlockSpec(memory_space=pltpu.VMEM)] * (len(args) - smem)
    specs += [pl.BlockSpec(memory_space=pl.ANY)] * len(after)
    first, last = len(args), len(args) + len(after)
    args = tuple(args) + tuple(after)
    body = kernel

    def kernel(*refs):
        body(*refs[:first], *refs[last:])
    return pl.pallas_call(
        kernel,
        name=name,
        out_shape=[jax.ShapeDtypeStruct(s, d) for s, d in outs],
        in_specs=specs,
        out_specs=[pl.BlockSpec(memory_space=pltpu.VMEM)] * len(outs),
        scratch_shapes=list(scratch),
        cost_estimate=cost(us),
        compiler_params=pltpu.CompilerParams(vmem_limit_bytes=VMEM),
    )(*args)


def routing_kernel(routes, routes_t, cot, pick, pick_t, mask_out, rows_out):
    lane = iota((ROWS, EXTRA), 1)
    mask = jnp.zeros((ROWS, EXTRA), f32)
    for k in range(TOP):
        mask += (routes[:, k : k + 1] == lane).astype(f32)
    sub = iota((OWNERS, ROWS), 0)
    mask_t = jnp.zeros((OWNERS, ROWS), f32)
    for k in range(TOP):
        mask_t += (routes_t[k : k + 1, :] == sub).astype(f32)
    mask_b = mask.astype(bf16)
    mask_tb = mask_t.astype(bf16)
    i0, i1 = iota((ROWS, ROWS), 0), iota((ROWS, ROWS), 1)
    before = nn((i1 < i0).astype(f32).astype(bf16), mask_b).astype(bf16)
    before_t = nn(mask_tb, (i0 < i1).astype(f32).astype(bf16)).astype(bf16)
    spread = ((iota((EXTRA, SLOTS), 1) // CAP) == iota((EXTRA, SLOTS), 0)).astype(f32).astype(bf16)
    spread_t = ((iota((SLOTS, OWNERS), 0) // CAP) == iota((SLOTS, OWNERS), 1)).astype(f32)
    spread_t = spread_t.astype(bf16)
    slot = (iota((ROWS, SLOTS), 1) % CAP).astype(f32)
    slot_t = (iota((SLOTS, ROWS), 0) % CAP).astype(f32)
    p = jnp.where(nn(before, spread) == slot, nn(mask_b, spread), 0.0)
    p_t = jnp.where(nn(spread_t, before_t) == slot_t, nn(spread_t, mask_tb), 0.0)
    pick[...] = p.astype(bf16)
    pick_t[...] = p_t.astype(bf16)
    mask_out[...] = mask
    p_tb = p_t.astype(bf16)
    rows_out[:, :WIDTH] = nn(p_tb, cot[...]).astype(bf16)
    rows_out[:, WIDTH:] = nn(p_tb, mask_b).astype(bf16)


def swap_halves(t):
    lane = iota(t.shape, 1) % 64
    return jnp.where(lane < 32, pltpu.roll(t, 96, 1), pltpu.roll(t, 32, 1))


def allowed(split, low, rows, keys):
    qi = iota((rows, keys), 0) + low
    kj = iota((rows, keys), 1)
    start = jnp.where(qi >= split, split, 0)
    return (kj <= qi) & (kj >= start)


BLOCK = 256
BLOCKS = GROUP // BLOCK


def head_place(h):
    return h // 2, h % 2, (h // 2) != (h % 2)


def source(z, d):
    return (z + LANES - d) % LANES


def rows_at(start, size, step):
    return pl.ds(pl.multiple_of(start, step), size)


def pack_kernel(place, w_query, w_key, w_value, w_router, gains, own, *sent):
    z, core = place[0], place[1]
    select = ((iota((16, EXTRA), 1) - OWNERS) == iota((16, EXTRA), 0)) & (iota((16, EXTRA), 0) < 2)
    small = tn(gains[...], select.astype(f32).astype(bf16)).astype(bf16)
    own[:, 512:640] = small
    own[:, 512 : 512 + OWNERS] = w_router[...]

    def columns(dest, rows):
        q = w_query[rows, rows_at(dest * 256, 256, 256)]
        k = w_key[rows, rows_at(dest * 128, 128, 128)]
        return q, k, w_value[rows, rows_at(dest * 128, 128, 128)]

    q, k, v = columns(z, slice(None))
    own[:, :256], own[:, 256:384], own[:, 384:512] = q, k, v
    half = rows_at(core * 128, 128, 128)
    for d, out in enumerate(sent):
        q, k, v = columns((z + d + 1) % LANES, half)
        out[:, :256], out[:, 256:384], out[:, 384:512] = q, k, v
        out[:, 512:640] = own[half, 512:640]


def gain_row(small, which):
    select = (iota((16, EXTRA), 1) == OWNERS + which).astype(f32).astype(bf16)
    return nt(select, small)[:1]


def front_kernel(
    split,
    place,
    x0,
    x1,
    x2,
    x3,
    w_own,
    w_mine,
    w_other,
    cosine,
    sine,
    x_ref,
    w_ref,
    normed,
    q_out,
    k_out,
    v_out,
    mixed,
    m0,
    m1,
    m2,
    m3,
):
    z, core = place[0], place[1]
    for d, piece in enumerate((x0, x1, x2, x3)):
        x_ref[rows_at(source(z, d) * ROWS, ROWS, 64), :] = piece[...]
    w_ref[rows_at(z * 256, 256, 256), :] = w_own[...]
    for d in (1, 2, 3):
        start = source(z, d) * 256
        w_ref[rows_at(start + core * 128, 128, 128), :] = w_mine[d - 1]
        w_ref[rows_at(start + (1 - core) * 128, 128, 128), :] = w_other[d - 1]
    x = x_ref[...].astype(f32)
    factor = lax.rsqrt(jnp.mean(x * x, axis=-1, keepdims=True) + epsilon)
    normed_b = (x * factor * gain_row(w_ref[:, 512:640], 0)).astype(bf16)
    normed[...] = normed_b
    lin = nn(normed_b, w_ref[:, :512])
    c, s = cosine[...], sine[...]
    for g in range(2):
        part = lin[:, 128 * g : 128 * g + 128]
        q_out[:, 128 * g : 128 * g + 128] = (part * c + swap_halves(part) * s).astype(bf16)
    part = lin[:, 256:384]
    key = part * c + swap_halves(part) * s
    key_b = key.astype(bf16)
    k_out[...] = key_b
    value_b = lin[:, 384:512].astype(bf16)
    v_out[...] = value_b
    keys = (key_b, pltpu.roll(key_b.astype(f32), 64, 1).astype(bf16))
    values = (value_b, pltpu.roll(value_b.astype(f32), 64, 1).astype(bf16))
    low_half = iota((BLOCK, 128), 1) < 64
    for i in range(BLOCKS):
        n = (i + 1) * BLOCK
        ok = allowed(split[0], i * BLOCK, BLOCK, n)
        for g in range(2):
            q2 = q_out[i * BLOCK : (i + 1) * BLOCK, 128 * g : 128 * g + 128].astype(f32) * score_scale
            halves = []
            for half in range(2):
                turned = g != half
                mine = low_half if half == 0 else ~low_half
                qh = jnp.where(mine, q2, 0.0).astype(bf16)
                scores = jnp.where(ok, nt(qh, keys[turned][:n]), -1e30)
                top = jnp.max(scores, axis=-1, keepdims=True)
                e = jnp.exp(scores - top)
                probs = (e / jnp.sum(e, axis=-1, keepdims=True)).astype(bf16)
                halves.append(nn(probs, values[turned][:n]))
            mixed[i * BLOCK : (i + 1) * BLOCK, 128 * g : 128 * g + 128] = jnp.where(
                low_half, halves[0], halves[1]
            ).astype(bf16)
    for d, out in enumerate((m0, m1, m2, m3)):
        out[...] = mixed[rows_at(((z + d) % LANES) * ROWS, ROWS, 64), :]


def middle_kernel(
    place,
    m0,
    m1,
    m2,
    m3,
    out_own,
    out_mine,
    out_other,
    x_ref,
    router,
    mask,
    pick_t,
    middle,
    second,
    gate,
    rows_out,
    w_out,
    mixed,
):
    z, core = place[0], place[1]
    for d, piece in enumerate((m0, m1, m2, m3)):
        mixed[:, rows_at(source(z, d) * 256, 256, 256)] = piece[...]
    w_out[rows_at(z * 256, 256, 256), :] = out_own[...]
    for d in (1, 2, 3):
        start = source(z, d) * 256
        w_out[rows_at(start + core * 128, 128, 128), :] = out_mine[d - 1]
        w_out[rows_at(start + (1 - core) * 128, 128, 128), :] = out_other[d - 1]
    mid = x_ref[...].astype(f32) + residual_scale * nn(mixed[...], w_out[...])
    middle[...] = mid
    factor = lax.rsqrt(jnp.mean(mid * mid, axis=-1, keepdims=True) + epsilon)
    second_b = (mid * factor * gain_row(router[...], 1)).astype(bf16)
    second[...] = second_b
    chosen = mask[...] > 0.5
    logits = jnp.where(chosen, nn(second_b, router[...]), -1e30)
    top = jnp.max(logits, axis=-1, keepdims=True)
    e = jnp.where(chosen, jnp.exp(logits - top), 0.0)
    gate[...] = e / jnp.sum(e, axis=-1, keepdims=True)
    rows_out[...] = nn(pick_t[...], second_b).astype(bf16)


EXPERT_BLOCK = 256


def expert_kernel(
    me, rows, h_up, mask, router, w_gate, w_up, *rest
):
    g_rows, hidden, g_gate, g_up, gate_out = rest[-5:]
    r = rows[...]
    lane = iota((EXPERT_BLOCK, EXTRA), 1)
    chosen = mask[...].astype(f32) > 0.5
    logits = jnp.where(chosen, nn(r, router[...]), -1e30)
    top = jnp.max(logits, axis=-1, keepdims=True)
    e = jnp.where(chosen, jnp.exp(logits - top), 0.0)
    total = jnp.sum(e, axis=-1, keepdims=True)
    mine = jnp.sum(jnp.where(lane == me[0], e, 0.0), axis=-1, keepdims=True)
    gate = mine / jnp.where(total > 0, total, 1.0)
    gate_out[...] = jnp.broadcast_to(gate, (EXPERT_BLOCK, EXTRA))
    gate_lin = nn(r, w_gate[...])
    up_lin = nn(r, w_up[...])
    sig = 1.0 / (1.0 + jnp.exp(-gate_lin))
    act = gate_lin * sig
    hidden_b = (act * up_lin).astype(bf16)
    hidden[...] = hidden_b
    up = h_up[...].astype(f32)
    g = residual_scale * jnp.sum(hidden_b.astype(f32) * up, axis=-1, keepdims=True)
    g_hidden = ((residual_scale * gate) * up).astype(bf16).astype(f32)
    gg = (g_hidden * up_lin * (sig * (1.0 + gate_lin * (1.0 - sig)))).astype(bf16)
    gu = (g_hidden * act).astype(bf16)
    g_gate[...] = gg
    g_up[...] = gu
    g_rows[:, :WIDTH] = (nt(gg, w_gate[...]) + nt(gu, w_up[...])).astype(bf16)
    high = g.astype(bf16).astype(f32)
    g_rows[:, WIDTH:] = jnp.where(
        lane == me[0], high, jnp.where(lane == me[0] + OWNERS, g - high, 0.0)
    ).astype(bf16)


def expert_call(me, rows, h_up, ups, router, w_gate, w_up, after):
    def whole(shape):
        return pl.BlockSpec(shape, lambda i: (0, 0))

    def blocked(width, column=0):
        return pl.BlockSpec((EXPERT_BLOCK, width), lambda i: (i, column))

    return pl.pallas_call(
        expert_kernel,
        name="expert",
        grid=(SLOTS // EXPERT_BLOCK,),
        out_shape=[
            jax.ShapeDtypeStruct((SLOTS, WIDTH + EXTRA), bf16),
            jax.ShapeDtypeStruct((SLOTS, FF), bf16),
            jax.ShapeDtypeStruct((SLOTS, FF), bf16),
            jax.ShapeDtypeStruct((SLOTS, FF), bf16),
            jax.ShapeDtypeStruct((SLOTS, EXTRA), f32),
        ],
        in_specs=[
            pl.BlockSpec(memory_space=pltpu.SMEM),
            blocked(WIDTH),
            blocked(FF),
            blocked(EXTRA, WIDTH // EXTRA),
            whole((WIDTH, EXTRA)),
            whole((WIDTH, FF)),
            whole((WIDTH, FF)),
        ]
        + [pl.BlockSpec(memory_space=pl.ANY)] * len(after),
        out_specs=[blocked(WIDTH + EXTRA), blocked(FF), blocked(FF), blocked(FF), blocked(EXTRA)],
        cost_estimate=cost(15),
        compiler_params=pltpu.CompilerParams(vmem_limit_bytes=60 * 1024 * 1024),
    )(me, rows, h_up, ups, router, w_gate, w_up, *after)


def return_kernel(
    place,
    back,
    pick,
    middle,
    second,
    gate,
    cot,
    router,
    w_out,
    g_middle_out,
    small_out,
    p0,
    p1,
    p2,
    p3,
    g_branch,
    g_mixed,
):
    ext = nn(pick[...], back[...])
    lane = iota((ROWS, EXTRA), 1)
    tail = ext[:, WIDTH:]
    g_gate = jnp.where(lane < OWNERS, tail + pltpu.roll(tail, EXTRA - OWNERS, 1), 0.0)
    probs = gate[...]
    g_logits = probs * (g_gate - jnp.sum(probs * g_gate, axis=-1, keepdims=True))
    high, low = split_two(g_logits)
    w = router[...]
    g_second = ext[:, :WIDTH] + (nt(high, w) + nt(low, w))
    mid = middle[...]
    factor = lax.rsqrt(jnp.mean(mid * mid, axis=-1, keepdims=True) + epsilon)
    z = mid * factor
    t = g_second * gain_row(w, 1)
    g_middle = cot[...].astype(f32) + factor * (t - z * jnp.mean(t * z, axis=-1, keepdims=True))
    g_middle_out[...] = g_middle
    branch_b = (residual_scale * g_middle).astype(bf16)
    g_branch[...] = branch_b
    g_mixed[...] = nt(branch_b, w_out[...]).astype(bf16)
    for d, out in enumerate((p0, p1, p2, p3)):
        there = rows_at(((place[0] + d) % LANES) * 256, 256, 256)
        out[:, :256] = g_mixed[:, there]
        out[:, 256:] = g_branch[:, there]
    s = second[...]
    one = (lane == OWNERS).astype(f32).astype(bf16)
    ph, plow = split_two(g_second * z)
    small_out[...] = tn(s, high) + tn(s, low) + tn(ph, one) + tn(plow, one)


def back_kernel(
    split,
    place,
    p0,
    p1,
    p2,
    p3,
    m0,
    m1,
    m2,
    m3,
    q_ref,
    k_ref,
    v_ref,
    normed,
    x_ref,
    w_ref,
    cosine,
    sine,
    small_in,
    keep,
    give,
    n0,
    n1,
    n2,
    n3,
    grads,
    g_normed_out,
    g_mixed,
    g_branch,
    g_query,
    g_key,
    g_value,
):
    z, core = place[0], place[1]
    for d, piece in enumerate((p0, p1, p2, p3)):
        rows = rows_at(source(z, d) * ROWS, ROWS, 64)
        g_mixed[rows, :] = piece[:, :256]
        g_branch[rows, :] = piece[:, 256:]
    key_b, value_b = k_ref[...], v_ref[...]
    keys = (key_b, pltpu.roll(key_b.astype(f32), 64, 1).astype(bf16))
    values = (value_b, pltpu.roll(value_b.astype(f32), 64, 1).astype(bf16))
    g_key[...] = jnp.zeros_like(g_key)
    g_value[...] = jnp.zeros_like(g_value)
    low_half = iota((BLOCK, 128), 1) < 64
    for i in range(BLOCKS):
        n = (i + 1) * BLOCK
        here = slice(i * BLOCK, (i + 1) * BLOCK)
        ok = allowed(split[0], i * BLOCK, BLOCK, n)
        for g in range(2):
            q2 = q_ref[here, 128 * g : 128 * g + 128].astype(f32) * score_scale
            gm2 = g_mixed[here, 128 * g : 128 * g + 128].astype(f32)
            halves = []
            for half in range(2):
                turned = int(g != half)
                mine = low_half if half == 0 else ~low_half
                qh = jnp.where(mine, q2, 0.0).astype(bf16)
                gm = jnp.where(mine, gm2, 0.0).astype(bf16)
                scores = jnp.where(ok, nt(qh, keys[turned][:n]), -1e30)
                top = jnp.max(scores, axis=-1, keepdims=True)
                e = jnp.exp(scores - top)
                probs = e / jnp.sum(e, axis=-1, keepdims=True)
                gp = nt(gm, values[turned][:n])
                pg = probs * gp
                gs = (pg - probs * jnp.sum(pg, axis=-1, keepdims=True)).astype(bf16)
                halves.append(nn(gs, keys[turned][:n]))
                g_key[turned, :n, :] += tn(gs, qh)
                g_value[turned, :n, :] += tn(probs.astype(bf16), gm)
            g_query[here, 128 * g : 128 * g + 128] = score_scale * jnp.where(
                low_half, halves[0], halves[1]
            )
    c, s = cosine[...], sine[...]

    def unturn(t):
        return (t * c - swap_halves(t) * s).astype(bf16)

    g_lin = jnp.concatenate(
        [
            unturn(g_query[:, :128]),
            unturn(g_query[:, 128:]),
            unturn(g_key[0] + pltpu.roll(g_key[1], 64, 1)),
            (g_value[0] + pltpu.roll(g_value[1], 64, 1)).astype(bf16),
        ],
        axis=1,
    )
    grads[:, :512] = tn(normed[...], g_lin).astype(bf16)
    for d, piece in enumerate((m0, m1, m2, m3)):
        grads[rows_at(source(z, d) * 256, 256, 256), 512:768] = tn(piece[...], g_branch[...]).astype(bf16)
    g_normed = nt(g_lin, w_ref[:, :512])
    g_normed_out[...] = g_normed.astype(bf16)
    x = x_ref[...].astype(f32)
    y = x * lax.rsqrt(jnp.mean(x * x, axis=-1, keepdims=True) + epsilon)
    one = (iota((GROUP, EXTRA), 1) == OWNERS + 1).astype(f32).astype(bf16)
    ph, plow = split_two(g_normed * y)
    grads[:, 768:] = (small_in[...] + tn(ph, one) + tn(plow, one)).astype(bf16)
    for a in range(LANES):
        keep[128 * a : 128 * a + 128, :] = grads[rows_at(a * 256 + core * 128, 128, 128), :]
        give[128 * a : 128 * a + 128, :] = grads[rows_at(a * 256 + (1 - core) * 128, 128, 128), :]
    for d, out in enumerate((n0, n1, n2, n3)):
        out[...] = g_normed_out[rows_at(((z + d) % LANES) * ROWS, ROWS, 64), :]


def add_kernel(a, b, out):
    out[...] = (a[...].astype(f32) + b[...].astype(f32)).astype(bf16)


def strip_kernel(arrived, out):
    total = jnp.sum(arrived[...].astype(f32).reshape(LANES, 16, 8, 768 + EXTRA), axis=1)
    parts = [total[a, :, :256] for a in range(LANES)]
    parts += [total[a, :, 256:384] for a in range(LANES)]
    parts += [total[a, :, 384:512] for a in range(LANES)]
    parts += [total[a, :, 512:768] for a in range(LANES)]
    strip = jnp.concatenate(parts + [jnp.sum(total[:, :, 768:], axis=0)], axis=1)
    out[...] = jnp.concatenate([strip] * 16, axis=0).astype(bf16)


def final_kernel(place, mine, other, query, key, value, out, router, gains):
    core = place[1]
    for piece, half in ((mine, core), (other, 1 - core)):
        rows = rows_at(half * 128, 128, 128)
        query[rows, :] = piece[:, :1024].astype(f32)
        key[rows, :] = piece[:, 1024:1536].astype(f32)
        value[rows, :] = piece[:, 1536:2048].astype(f32)
        out[rows, :] = piece[:, 2048:3072].astype(f32)
        router[rows, :] = piece[:, 3072 : 3072 + OWNERS].astype(f32)
        select = iota((16, EXTRA), 1) == iota((16, EXTRA), 0) + OWNERS
        gains[:, rows] = nt(select.astype(f32).astype(bf16), piece[:, 3072:])


def z_shift(value, d):
    return lax.ppermute(value, "wshard", [(i, (i + d) % LANES) for i in range(LANES)])


def z_shifts(values):
    return [z_shift(v, d) for d, v in zip((1, 2, 3), values)]


def other_core(value):
    return lax.ppermute(value, "expert", [(i, i ^ 1) for i in range(OWNERS)])


def to_owners(value):
    return lax.all_to_all(value, "expert", 0, 0, tiled=True)


def local(
    tokens,
    w_query,
    w_key,
    w_value,
    w_out,
    w_router,
    gain_attn,
    gain_moe,
    w_gate,
    w_up,
    w_down,
    routes,
    seq_split,
    cotangent,
):
    z = lax.axis_index("wshard")
    me = lax.axis_index("expert")
    core = me % 2
    place = jnp.stack([z, core]).astype(jnp.int32)
    w_gate, w_up, w_down = w_gate[0], w_up[0], w_down[0]

    gains = jnp.zeros((16, 256), bf16).at[0].set(gain_attn).at[1].set(gain_moe)
    w_own, *w_sent = call(
        pack_kernel,
        "pack",
        [((256, 640), bf16)] + [((128, 640), bf16)] * 3,
        (place, w_query, w_key, w_value, w_router, gains),
        1,
        smem=1,
    )
    w_mine = jnp.stack(z_shifts(w_sent))
    w_other = other_core(w_mine)
    x_pieces = [tokens] + z_shifts([tokens] * 3)

    pick, pick_t, mask, ups_send = call(
        routing_kernel,
        "routing",
        [
            ((ROWS, SLOTS), bf16),
            ((SLOTS, ROWS), bf16),
            ((ROWS, EXTRA), f32),
            ((SLOTS, WIDTH + EXTRA), bf16),
        ],
        (routes, routes.T, cotangent),
        5,
    )
    ups = to_owners(ups_send.reshape(OWNERS, CAP, WIDTH + EXTRA)).reshape(SLOTS, WIDTH + EXTRA)

    half_out = lax.dynamic_slice(w_out, (core * 128, 0), (128, WIDTH))
    out_mine = jnp.stack(z_shifts([half_out] * 3))
    out_other = other_core(out_mine)

    split_at = seq_split[0]
    places = jnp.arange(GROUP, dtype=jnp.int32)
    position = jnp.where(places >= split_at, places - split_at, places).astype(f32)
    exponent = jnp.arange(32, dtype=f32) * (2.0 / 64)
    angles = position[:, None] * jnp.power(rope_base, -exponent)[None, :]
    cosine, sine = jnp.cos(angles), jnp.sin(angles)
    cosine = jnp.concatenate([cosine] * 4, axis=1)
    sine = jnp.concatenate([-sine, sine] * 2, axis=1)

    x_all, w_all, normed, query, key, value, mixed, *mixed_sent = call(
        front_kernel,
        "attention",
        [
            ((GROUP, WIDTH), bf16),
            ((WIDTH, 640), bf16),
            ((GROUP, WIDTH), bf16),
            ((GROUP, 256), bf16),
            ((GROUP, 128), bf16),
            ((GROUP, 128), bf16),
            ((GROUP, 256), bf16),
        ]
        + [((ROWS, 256), bf16)] * 4,
        (seq_split, place, *x_pieces, w_own, w_mine, w_other, cosine, sine),
        80,
        smem=2,
    )
    small_all = w_all[:, 512:]
    middle, second, gate, rows_send, out_all = call(
        middle_kernel,
        "middle",
        [
            ((ROWS, WIDTH), f32),
            ((ROWS, WIDTH), bf16),
            ((ROWS, EXTRA), f32),
            ((SLOTS, WIDTH), bf16),
            ((WIDTH, WIDTH), bf16),
        ],
        (
            place,
            mixed_sent[0],
            *z_shifts(mixed_sent[1:]),
            w_out,
            out_mine,
            out_other,
            tokens,
            small_all,
            mask,
            pick_t,
        ),
        6,
        smem=1,
        scratch=[pltpu.VMEM((ROWS, WIDTH), bf16)],
    )
    rows_in = to_owners(rows_send.reshape(OWNERS, CAP, WIDTH)).reshape(SLOTS, WIDTH)
    mixed_pieces = [mixed] + z_shifts([mixed] * 3)

    up_rows = ups[:, :WIDTH]
    h_up = nt(up_rows, w_down).astype(bf16)
    g_rows, hidden, g_gate, g_up, gate_rows = expert_call(
        me.reshape(1), rows_in, h_up, ups, small_all, w_gate, w_up, mixed_pieces
    )
    back = to_owners(g_rows.reshape(OWNERS, CAP, WIDTH + EXTRA)).reshape(SLOTS, WIDTH + EXTRA)

    row_gate = gate_rows[:, :1]
    g_out = (residual_scale * row_gate * up_rows.astype(f32)).astype(bf16)
    gate_grad = tn(rows_in, g_gate).astype(bf16)
    up_grad = tn(rows_in, g_up).astype(bf16)
    down_grad = tn(hidden, g_out).astype(bf16)

    def shared_sum(grad):
        parts = grad.reshape(LANES, -1, grad.shape[1])

        def part(d):
            return lax.dynamic_index_in_dim(parts, (z + d) % LANES, 0, keepdims=False)

        total = part(0).astype(f32)
        for piece in z_shifts([part(d) for d in (1, 2, 3)]):
            total += piece.astype(f32)
        return total

    gate_share, up_share, down_share = (shared_sum(g) for g in (gate_grad, up_grad, down_grad))
    expert_out = nn(hidden, w_down).astype(bf16).astype(f32)
    out_back = to_owners((row_gate * expert_out).astype(bf16).reshape(OWNERS, CAP, WIDTH))

    g_middle, small_grad, *branch_sent = call(
        return_kernel,
        "return",
        [((ROWS, WIDTH), f32), ((WIDTH, EXTRA), f32)] + [((ROWS, 512), bf16)] * 4,
        (place, back, pick, middle, second, gate, cotangent, small_all, out_all),
        7,
        smem=1,
        scratch=[pltpu.VMEM((ROWS, WIDTH), bf16), pltpu.VMEM((ROWS, WIDTH), bf16)],
        after=(gate_share, up_share, down_share),
    )
    wide = 768 + EXTRA
    keep, give, *normed_sent = call(
        back_kernel,
        "attention_back",
        [((512, wide), bf16)] * 2 + [((ROWS, WIDTH), bf16)] * 4,
        (
            seq_split,
            place,
            branch_sent[0],
            *z_shifts(branch_sent[1:]),
            *mixed_pieces,
            query,
            key,
            value,
            normed,
            x_all,
            w_all,
            cosine,
            sine,
            small_grad,
        ),
        18,
        smem=2,
        scratch=[
            pltpu.VMEM((WIDTH, wide), bf16),
            pltpu.VMEM((GROUP, WIDTH), bf16),
            pltpu.VMEM((GROUP, 256), bf16),
            pltpu.VMEM((GROUP, 256), bf16),
            pltpu.VMEM((GROUP, 256), f32),
            pltpu.VMEM((2, GROUP, 128), f32),
            pltpu.VMEM((2, GROUP, 128), f32),
        ],
    )

    output = middle + residual_scale * nn(pick, out_back.reshape(SLOTS, WIDTH))

    g_own = normed_sent[0].astype(f32)
    for piece in z_shifts(normed_sent[1:]):
        g_own += piece.astype(f32)
    x = tokens.astype(f32)
    factor = lax.rsqrt(jnp.mean(x * x, axis=-1, keepdims=True) + epsilon)
    y = x * factor
    t = g_own * small_all[:, OWNERS].astype(f32)[None, :]
    input_grad = g_middle + factor * (t - y * jnp.mean(t * y, axis=-1, keepdims=True))

    chip = call(
        add_kernel, "add", [((512, wide), bf16)], (keep, other_core(give)), 1, after=(out_back,)
    )[0]
    groups = [
        [(2 * xy + c) * LANES + a for a in range(LANES) for xy in range(OWNERS // 2)]
        for c in range(2)
    ]
    arrived = lax.all_to_all(
        chip.reshape(64, 8, wide),
        ("expert", "wshard"),
        0,
        0,
        tiled=True,
        axis_index_groups=groups,
    )
    strips = call(
        strip_kernel,
        "strip",
        [((128, 3072 + EXTRA), bf16)],
        (arrived.reshape(512, wide),),
        2,
        after=(output, input_grad),
    )[0]
    shared = lax.all_to_all(
        strips.reshape(OWNERS // 2, 8, 3072 + EXTRA),
        "expert",
        0,
        0,
        tiled=True,
        axis_index_groups=[[2 * xy + c for xy in range(OWNERS // 2)] for c in range(2)],
    ).reshape(128, 3072 + EXTRA)
    grad_query, grad_key, grad_value, grad_out, grad_router, grad_gains = call(
        final_kernel,
        "final",
        [
            ((256, 1024), f32),
            ((256, 512), f32),
            ((256, 512), f32),
            ((256, 1024), f32),
            ((256, OWNERS), f32),
            ((16, 256), f32),
        ],
        (place, shared, other_core(shared)),
        2,
        smem=1,
    )

    return (
        output,
        input_grad,
        grad_query,
        grad_key,
        grad_value,
        grad_out,
        grad_router,
        grad_gains[1],
        grad_gains[0],
        gate_share[None],
        up_share[None],
        down_share[None],
    )


def solution(mesh):
    rows = P(("expert", "wshard"), None)
    dense = P("wshard", None)
    expert = P("expert", None, None)
    shard = P("expert", "wshard", None)
    in_specs = (rows,) + (dense,) * 5 + (P("wshard"),) * 2 + (expert,) * 3
    in_specs += (rows, P("expert"), rows)
    out_specs = (rows, rows) + (dense,) * 5 + (P("wshard"),) * 2 + (shard,) * 3
    return jax.shard_map(local, mesh=mesh, in_specs=in_specs, out_specs=out_specs, check_vma=False)
```

```python
import functools

import jax
import jax.numpy as jnp
from jax import lax
from jax.experimental import pallas as pl
from jax.experimental.pallas import tpu as pltpu
from jax.sharding import PartitionSpec as P

f32 = jnp.float32
bf16 = jnp.bfloat16
epsilon = 1e-06
residual_scale = 0.22
score_scale = 0.015625
rope_base = 10000.0

LANES = 4
OWNERS = 32
ROWS = 192
GROUP = 768
WIDTH = 1024
CAP = 64
SLOTS = OWNERS * CAP
FF = 512
TOP = 8
EXTRA = 128
VMEM = 50 * 1024 * 1024
ALL_VMEM = 60 * 1024 * 1024


def nn(a, b):
    return lax.dot_general(a, b, (((1,), (0,)), ((), ())), preferred_element_type=f32)


def nt(a, b):
    return lax.dot_general(a, b, (((1,), (1,)), ((), ())), preferred_element_type=f32)


def tn(a, b):
    return lax.dot_general(a, b, (((0,), (0,)), ((), ())), preferred_element_type=f32)


def iota(shape, axis):
    return lax.broadcasted_iota(jnp.int32, shape, axis)


def split_two(v):
    high = v.astype(bf16)
    return high, (v - high.astype(f32)).astype(bf16)


def cost(us):
    return pl.CostEstimate(
        flops=int(us * 1e9), bytes_accessed=int(us * 3.5e6), transcendentals=0
    )


def call(kernel, name, outs, args, us, smem=0, scratch=(), after=(), vmem=VMEM):
    specs = [pl.BlockSpec(memory_space=pltpu.SMEM)] * smem
    specs += [pl.BlockSpec(memory_space=pltpu.VMEM)] * (len(args) - smem)
    specs += [pl.BlockSpec(memory_space=pltpu.HBM)] * len(after)
    first, last = len(args), len(args) + len(after)
    args = tuple(args) + tuple(after)
    body = kernel

    def kernel(*refs):
        body(*refs[:first], *refs[last:])
    return pl.pallas_call(
        kernel,
        name=name,
        out_shape=[jax.ShapeDtypeStruct(s, d) for s, d in outs],
        in_specs=specs,
        out_specs=[pl.BlockSpec(memory_space=pltpu.VMEM)] * len(outs),
        scratch_shapes=list(scratch),
        cost_estimate=cost(us),
        compiler_params=pltpu.CompilerParams(vmem_limit_bytes=vmem),
    )(*args)


def spread_rows():
    same = (iota((SLOTS, EXTRA), 0) // CAP) == iota((SLOTS, EXTRA), 1)
    return same.astype(f32).astype(bf16)


def earlier():
    return (iota((ROWS, ROWS), 0) < iota((ROWS, ROWS), 1)).astype(f32).astype(bf16)


def routing_kernel(routes_t, cot, pick_t, rows_out):
    sub = iota((EXTRA, ROWS), 0)
    mask_t = jnp.zeros((EXTRA, ROWS), f32)
    for k in range(TOP):
        mask_t += (routes_t[k : k + 1, :] == sub).astype(f32)
    mask_tb = mask_t.astype(bf16)
    before_t = nn(mask_tb, earlier())
    slot = iota((CAP, ROWS), 0).astype(f32)
    p_t = jnp.concatenate(
        [
            jnp.where(before_t[e : e + 1] == slot, mask_t[e : e + 1], 0.0).astype(bf16)
            for e in range(OWNERS)
        ],
        axis=0,
    )
    pick_t[...] = p_t
    rows_out[:, :WIDTH] = nn(p_t, cot[...]).astype(bf16)
    rows_out[:, WIDTH:] = nt(p_t, mask_tb).astype(bf16)


def mask_kernel(routes, pick, mask_out):
    lane = iota((ROWS, EXTRA), 1)
    mask = jnp.zeros((ROWS, EXTRA), f32)
    for k in range(TOP):
        mask += (routes[:, k : k + 1] == lane).astype(f32)
    mask_out[...] = mask
    mask_b = mask.astype(bf16)
    before = tn(earlier(), mask_b).astype(bf16)
    spread = spread_rows()
    slot = (iota((ROWS, SLOTS), 1) % CAP).astype(f32)
    pick[...] = jnp.where(nt(before, spread) == slot, nt(mask_b, spread), 0.0).astype(bf16)


def gate_kernel(gate, pick, weights):
    spread = spread_rows()
    high, low = split_two(gate[...])
    w = pick[...].astype(f32) * (nt(high, spread) + nt(low, spread))
    weights[...] = w.astype(bf16)


def swap_halves(t):
    lane = iota(t.shape, 1) % 64
    return jnp.where(lane < 32, pltpu.roll(t, 96, 1), pltpu.roll(t, 32, 1))


def allowed(split, low, rows, keys):
    qi = iota((rows, keys), 0) + low
    kj = iota((rows, keys), 1)
    start = jnp.where(qi >= split, split, 0)
    return (kj <= qi) & (kj >= start)


BLOCK = 256
BLOCKS = GROUP // BLOCK


def head_place(h):
    return h // 2, h % 2, (h // 2) != (h % 2)


def source(z, d):
    return (z + LANES - d) % LANES


def rows_at(start, size, step):
    return pl.ds(pl.multiple_of(start, step), size)


def pack_kernel(place, w_query, w_key, w_value, w_router, gains, own, *sent):
    z, core = place[0], place[1]
    select = ((iota((16, EXTRA), 1) - OWNERS) == iota((16, EXTRA), 0)) & (iota((16, EXTRA), 0) < 2)
    small = tn(gains[...], select.astype(f32).astype(bf16)).astype(bf16)
    own[:, 512:640] = small
    own[:, 512 : 512 + OWNERS] = w_router[...]

    def fill(out, dest, rows):
        out[:, :256] = w_query[rows, rows_at(dest * 256, 256, 256)]
        out[:, 256:384] = w_key[rows, rows_at(dest * 128, 128, 128)]
        out[:, 384:512] = w_value[rows, rows_at(dest * 128, 128, 128)]

    fill(own, z, slice(None))
    half = rows_at(core * 128, 128, 128)
    for d, out in enumerate(sent):
        fill(out, (z + d + 1) % LANES, half)
        out[:, 512:640] = own[half, 512:640]


def norm_kernel(place, x0, x1, x2, x3, x_ref, factor):
    for d, piece in enumerate((x0, x1, x2, x3)):
        x_ref[rows_at(source(place[0], d) * ROWS, ROWS, 64), :] = piece[...]
    x = x_ref[...].astype(f32)
    r = lax.rsqrt(jnp.mean(x * x, axis=-1, keepdims=True) + epsilon)
    factor[...] = jnp.broadcast_to(r, (GROUP, EXTRA))


def gain_row(small, which):
    select = (iota((16, EXTRA), 1) == OWNERS + which).astype(f32).astype(bf16)
    return nt(select, small)[:1]


def front_kernel(
    split,
    place,
    x_ref,
    factor,
    w_own,
    w_mine,
    w_other,
    cosine,
    sine,
    w_ref,
    normed,
    q_out,
    k_out,
    v_out,
    mixed,
    m0,
    m1,
    m2,
    m3,
):
    z, core = place[0], place[1]
    w_ref[rows_at(z * 256, 256, 256), :] = w_own[...]
    for d in (1, 2, 3):
        start = source(z, d) * 256
        w_ref[rows_at(start + core * 128, 128, 128), :] = w_mine[d - 1]
        w_ref[rows_at(start + (1 - core) * 128, 128, 128), :] = w_other[d - 1]
    x = x_ref[...].astype(f32)
    normed_b = (x * factor[:, :1] * gain_row(w_ref[:, 512:640], 0)).astype(bf16)
    normed[...] = normed_b
    lin = nn(normed_b, w_ref[:, :512])
    c, s = cosine[...], sine[...]
    for g in range(2):
        part = lin[:, 128 * g : 128 * g + 128]
        q_out[:, 128 * g : 128 * g + 128] = (part * c + swap_halves(part) * s).astype(bf16)
    part = lin[:, 256:384]
    key = part * c + swap_halves(part) * s
    key_b = key.astype(bf16)
    k_out[...] = key_b
    value_b = lin[:, 384:512].astype(bf16)
    v_out[...] = value_b
    keys = (key_b, pltpu.roll(key_b.astype(f32), 64, 1).astype(bf16))
    values = (value_b, pltpu.roll(value_b.astype(f32), 64, 1).astype(bf16))
    low_half = iota((BLOCK, 128), 1) < 64
    for i in range(BLOCKS):
        n = (i + 1) * BLOCK
        ok = allowed(split[0], i * BLOCK, BLOCK, n)
        for g in range(2):
            q2 = q_out[i * BLOCK : (i + 1) * BLOCK, 128 * g : 128 * g + 128].astype(f32) * score_scale
            halves = []
            for half in range(2):
                turned = g != half
                mine = low_half if half == 0 else ~low_half
                qh = jnp.where(mine, q2, 0.0).astype(bf16)
                scores = jnp.where(ok, nt(qh, keys[turned][:n]), -1e30)
                top = jnp.max(scores, axis=-1, keepdims=True)
                e = jnp.exp(scores - top)
                share = 1.0 / jnp.sum(e, axis=-1, keepdims=True)
                halves.append(share * nn(e.astype(bf16), values[turned][:n]))
            mixed[i * BLOCK : (i + 1) * BLOCK, 128 * g : 128 * g + 128] = jnp.where(
                low_half, halves[0], halves[1]
            ).astype(bf16)
    for d, out in enumerate((m0, m1, m2, m3)):
        out[...] = mixed[rows_at(((z + d) % LANES) * ROWS, ROWS, 64), :]


def middle_kernel(
    place,
    m0,
    m1,
    m2,
    m3,
    out_own,
    out_mine,
    out_other,
    x_ref,
    router,
    mask,
    pick_t,
    middle,
    second,
    gate,
    rows_out,
    w_out,
    mixed,
):
    z, core = place[0], place[1]
    for d, piece in enumerate((m0, m1, m2, m3)):
        mixed[:, rows_at(source(z, d) * 256, 256, 256)] = piece[...]
    w_out[rows_at(z * 256, 256, 256), :] = out_own[...]
    for d in (1, 2, 3):
        start = source(z, d) * 256
        w_out[rows_at(start + core * 128, 128, 128), :] = out_mine[d - 1]
        w_out[rows_at(start + (1 - core) * 128, 128, 128), :] = out_other[d - 1]
    mid = x_ref[...].astype(f32) + residual_scale * nn(mixed[...], w_out[...])
    middle[...] = mid
    factor = lax.rsqrt(jnp.mean(mid * mid, axis=-1, keepdims=True) + epsilon)
    second_b = (mid * factor * gain_row(router[...], 1)).astype(bf16)
    second[...] = second_b
    chosen = mask[...] > 0.5
    logits = jnp.where(chosen, nn(second_b, router[...]), -1e30)
    top = jnp.max(logits, axis=-1, keepdims=True)
    e = jnp.where(chosen, jnp.exp(logits - top), 0.0)
    gate[...] = e / jnp.sum(e, axis=-1, keepdims=True)
    rows_out[...] = nn(pick_t[...], second_b).astype(bf16)


EXPERT_BLOCK = 512
PARTS = WIDTH // 128
PACKED = PARTS * CAP + 16


def expert_kernel(rows, h_up, w_gate, w_up, *rest):
    g_rows, hidden, g_gate, g_up = rest[-4:]
    r = rows[...]
    gate_lin = nn(r, w_gate[...])
    up_lin = nn(r, w_up[...])
    sig = 1.0 / (1.0 + jnp.exp(-gate_lin))
    act = gate_lin * sig
    hidden_b = (act * up_lin).astype(bf16)
    hidden[...] = hidden_b
    g_hidden = h_up[...].astype(f32)
    g = jnp.sum(hidden_b.astype(f32) * g_hidden, axis=-1, keepdims=True)
    gg = (g_hidden * up_lin * (sig * (1.0 + gate_lin * (1.0 - sig)))).astype(bf16)
    gu = (g_hidden * act).astype(bf16)
    g_gate[...] = gg
    g_up[...] = gu
    result = (nt(gg, w_gate[...]) + nt(gu, w_up[...])).astype(bf16)
    lane, slot = iota((CAP, 128), 1), iota((CAP, 128), 0)
    high = g.astype(bf16).astype(f32)
    for s in range(EXPERT_BLOCK // CAP):
        here = slice(CAP * s, CAP * s + CAP)
        for j in range(PARTS):
            g_rows[s, CAP * j : CAP * j + CAP, :] = result[here, 128 * j : 128 * j + 128]
        spread = jnp.where(
            lane == slot,
            high[here],
            jnp.where(lane == slot + CAP, (g - high)[here], 0.0),
        )
        scalars = jnp.sum(spread, axis=0, keepdims=True)
        g_rows[s, PARTS * CAP :, :] = jnp.broadcast_to(scalars, (16, 128)).astype(bf16)


def row_gate_kernel(me, rows, mask, router, out):
    chosen = mask[...].astype(f32) > 0.5
    logits = jnp.where(chosen, nn(rows[...], router[...]), -1e30)
    top = jnp.max(logits, axis=-1, keepdims=True)
    e = jnp.where(chosen, jnp.exp(logits - top), 0.0)
    total = jnp.sum(e, axis=-1, keepdims=True)
    mine = jnp.sum(jnp.where(iota((SLOTS, EXTRA), 1) == me[0], e, 0.0), axis=-1, keepdims=True)
    out[...] = jnp.broadcast_to(mine / jnp.where(total > 0, total, 1.0), (SLOTS, EXTRA))


def hold_kernel(value, out):
    out[...] = value[...]


def stack_kernel(a, b, c, out):
    out[0], out[1], out[2] = a[...], b[...], c[...]


def expert_call(rows, h_up, w_gate, w_up, after):
    def whole(shape):
        return pl.BlockSpec(shape, lambda i: (0, 0))

    def blocked(width):
        return pl.BlockSpec((EXPERT_BLOCK, width), lambda i: (i, 0))

    return pl.pallas_call(
        expert_kernel,
        name="expert",
        grid=(SLOTS // EXPERT_BLOCK,),
        out_shape=[jax.ShapeDtypeStruct((OWNERS, PACKED, 128), bf16)]
        + [jax.ShapeDtypeStruct((SLOTS, FF), bf16)] * 3,
        in_specs=[blocked(WIDTH), blocked(FF), whole((WIDTH, FF)), whole((WIDTH, FF))]
        + [pl.BlockSpec(memory_space=pltpu.HBM)] * len(after),
        out_specs=[pl.BlockSpec((EXPERT_BLOCK // CAP, PACKED, 128), lambda i: (i, 0, 0))]
        + [blocked(FF)] * 3,
        cost_estimate=cost(15),
        compiler_params=pltpu.CompilerParams(vmem_limit_bytes=60 * 1024 * 1024),
    )(rows, h_up, w_gate, w_up, *after)


def return_kernel(
    place,
    back,
    pick,
    weights,
    middle,
    second,
    gate,
    cot,
    router,
    w_out,
    g_middle_out,
    small_out,
    p0,
    p1,
    p2,
    p3,
    g_branch,
    g_mixed,
):
    lane = iota((ROWS, EXTRA), 1)
    spread = spread_rows()
    scalars = nn(spread[:, :OWNERS], back[:, PARTS * CAP, :])
    offset, lanes = iota((SLOTS, EXTRA), 0) % CAP, iota((SLOTS, EXTRA), 1)
    column = jnp.sum(jnp.where(lanes % CAP == offset, scalars, 0.0), axis=-1, keepdims=True)
    high, low = split_two(spread.astype(f32) * column)
    g_gate = nn(pick[...], high) + nn(pick[...], low)
    probs = gate[...]
    g_logits = probs * (g_gate - jnp.sum(probs * g_gate, axis=-1, keepdims=True))
    high, low = split_two(g_logits)
    w = router[...]
    pieces = [
        back[:, CAP * j : CAP * j + CAP, :].reshape(SLOTS, 128) for j in range(PARTS)
    ]
    summed = [
        nn(weights[...], jnp.concatenate(pieces[j : j + 2], axis=1)) for j in range(0, PARTS, 2)
    ]
    g_second = jnp.concatenate(summed, axis=1) + (nt(high, w) + nt(low, w))
    mid = middle[...]
    factor = lax.rsqrt(jnp.mean(mid * mid, axis=-1, keepdims=True) + epsilon)
    z = mid * factor
    t = g_second * gain_row(w, 1)
    g_middle = cot[...].astype(f32) + factor * (t - z * jnp.mean(t * z, axis=-1, keepdims=True))
    g_middle_out[...] = g_middle
    branch_b = (residual_scale * g_middle).astype(bf16)
    g_branch[...] = branch_b
    g_mixed[...] = nt(branch_b, w_out[...]).astype(bf16)
    for d, out in enumerate((p0, p1, p2, p3)):
        there = rows_at(((place[0] + d) % LANES) * 256, 256, 256)
        out[:, :256] = g_mixed[:, there]
        out[:, 256:] = g_branch[:, there]
    s = second[...]
    one = (lane == OWNERS).astype(f32).astype(bf16)
    ph, plow = split_two(g_second * z)
    small_out[...] = tn(s, high) + tn(s, low) + tn(ph, one) + tn(plow, one)


def back_kernel(
    split,
    place,
    p0,
    p1,
    p2,
    p3,
    m0,
    m1,
    m2,
    m3,
    q_ref,
    k_ref,
    v_ref,
    normed,
    x_ref,
    w_ref,
    cosine,
    sine,
    small_in,
    keep,
    give,
    n0,
    n1,
    n2,
    n3,
    grads,
    g_normed_out,
    g_mixed,
    g_branch,
    g_query,
    g_key,
    g_value,
):
    z, core = place[0], place[1]
    for d, piece in enumerate((p0, p1, p2, p3)):
        rows = rows_at(source(z, d) * ROWS, ROWS, 64)
        g_mixed[rows, :] = piece[:, :256]
        g_branch[rows, :] = piece[:, 256:]
    key_b, value_b = k_ref[...], v_ref[...]
    keys = (key_b, pltpu.roll(key_b.astype(f32), 64, 1).astype(bf16))
    values = (value_b, pltpu.roll(value_b.astype(f32), 64, 1).astype(bf16))
    g_key[...] = jnp.zeros_like(g_key)
    g_value[...] = jnp.zeros_like(g_value)
    low_half = iota((BLOCK, 128), 1) < 64
    for i in range(BLOCKS):
        n = (i + 1) * BLOCK
        here = slice(i * BLOCK, (i + 1) * BLOCK)
        ok = allowed(split[0], i * BLOCK, BLOCK, n)
        for g in range(2):
            q2 = q_ref[here, 128 * g : 128 * g + 128].astype(f32) * score_scale
            gm2 = g_mixed[here, 128 * g : 128 * g + 128].astype(f32)
            halves = []
            for half in range(2):
                turned = int(g != half)
                mine = low_half if half == 0 else ~low_half
                qh = jnp.where(mine, q2, 0.0).astype(bf16)
                gm = jnp.where(mine, gm2, 0.0).astype(bf16)
                scores = jnp.where(ok, nt(qh, keys[turned][:n]), -1e30)
                top = jnp.max(scores, axis=-1, keepdims=True)
                e = jnp.exp(scores - top)
                share = 1.0 / jnp.sum(e, axis=-1, keepdims=True)
                gp = nt(gm, values[turned][:n])
                mean = share * jnp.sum(e * gp, axis=-1, keepdims=True)
                gs = (e * (gp - mean)).astype(bf16)
                halves.append(share * nn(gs, keys[turned][:n]))
                g_key[turned, :n, :] += tn(gs, (share * qh.astype(f32)).astype(bf16))
                g_value[turned, :n, :] += tn(e.astype(bf16), (share * gm.astype(f32)).astype(bf16))
            g_query[here, 128 * g : 128 * g + 128] = score_scale * jnp.where(
                low_half, halves[0], halves[1]
            )
    c, s = cosine[...], sine[...]

    def unturn(t):
        return (t * c - swap_halves(t) * s).astype(bf16)

    g_lin = jnp.concatenate(
        [
            unturn(g_query[:, :128]),
            unturn(g_query[:, 128:]),
            unturn(g_key[0] + pltpu.roll(g_key[1], 64, 1)),
            (g_value[0] + pltpu.roll(g_value[1], 64, 1)).astype(bf16),
        ],
        axis=1,
    )
    grads[:, :512] = tn(normed[...], g_lin).astype(bf16)
    for d, piece in enumerate((m0, m1, m2, m3)):
        grads[rows_at(source(z, d) * 256, 256, 256), 512:768] = tn(piece[...], g_branch[...]).astype(bf16)
    g_normed = nt(g_lin, w_ref[:, :512])
    g_normed_out[...] = g_normed.astype(bf16)
    x = x_ref[...].astype(f32)
    y = x * lax.rsqrt(jnp.mean(x * x, axis=-1, keepdims=True) + epsilon)
    one = (iota((GROUP, EXTRA), 1) == OWNERS + 1).astype(f32).astype(bf16)
    ph, plow = split_two(g_normed * y)
    grads[:, 768:] = (small_in[...] + tn(ph, one) + tn(plow, one)).astype(bf16)
    for a in range(LANES):
        keep[128 * a : 128 * a + 128, :] = grads[rows_at(a * 256 + core * 128, 128, 128), :]
        give[128 * a : 128 * a + 128, :] = grads[rows_at(a * 256 + (1 - core) * 128, 128, 128), :]
    for d, out in enumerate((n0, n1, n2, n3)):
        out[...] = g_normed_out[rows_at(((z + d) % LANES) * ROWS, ROWS, 64), :]


def add_kernel(a, b, out):
    out[...] = (a[...].astype(f32) + b[...].astype(f32)).astype(bf16)


def strip_kernel(arrived, out):
    total = jnp.sum(arrived[...].astype(f32).reshape(LANES, 16, 8, 768 + EXTRA), axis=1)
    parts = [total[a, :, :256] for a in range(LANES)]
    parts += [total[a, :, 256:384] for a in range(LANES)]
    parts += [total[a, :, 384:512] for a in range(LANES)]
    parts += [total[a, :, 512:768] for a in range(LANES)]
    strip = jnp.concatenate(parts + [jnp.sum(total[:, :, 768:], axis=0)], axis=1)
    out[...] = jnp.concatenate([strip] * 16, axis=0).astype(bf16)


def final_kernel(place, piece, *refs):
    query, key, value, out, router, gain_m, gain_a = refs[-7:]
    query[...] = piece[:, :1024].astype(f32)
    key[...] = piece[:, 1024:1536].astype(f32)
    value[...] = piece[:, 1536:2048].astype(f32)
    out[...] = piece[:, 2048:3072].astype(f32)
    router[...] = piece[:, 3072 : 3072 + OWNERS].astype(f32)
    select = iota((16, EXTRA), 1) == iota((16, EXTRA), 0) + OWNERS
    gains = nt(select.astype(f32).astype(bf16), piece[:, 3072:])
    gain_m[...] = gains[0:1]
    gain_a[...] = gains[1:2]


def final_call(half, place, piece, before):
    def rows(width):
        return pl.BlockSpec((128, width), lambda i, p: ((p[1] + half) % 2, 0))

    def columns():
        return pl.BlockSpec((1, 128), lambda i, p: (0, (p[1] + half) % 2))

    widths = (1024, 512, 512, 1024, OWNERS)
    shapes = [(256, w) for w in widths] + [(1, 256)] * 2
    return pl.pallas_call(
        final_kernel,
        name="final",
        out_shape=[jax.ShapeDtypeStruct(s, f32) for s in shapes],
        grid_spec=pltpu.PrefetchScalarGridSpec(
            num_scalar_prefetch=1,
            grid=(1,),
            in_specs=[pl.BlockSpec((128, 3072 + EXTRA), lambda i, p: (0, 0))]
            + [pl.BlockSpec(memory_space=pltpu.HBM)] * len(before),
            out_specs=[rows(w) for w in widths] + [columns(), columns()],
        ),
        input_output_aliases={2 + i: i for i in range(len(before))},
        cost_estimate=cost(1),
        compiler_params=pltpu.CompilerParams(vmem_limit_bytes=VMEM),
    )(place, piece, *before)


def z_shift(value, d):
    return lax.ppermute(value, "wshard", [(i, (i + d) % LANES) for i in range(LANES)])


def z_shifts(values):
    return [z_shift(v, d) for d, v in zip((1, 2, 3), values)]


def other_core(value):
    return lax.ppermute(value, "expert", [(i, i ^ 1) for i in range(OWNERS)])


def to_owners(value):
    return lax.all_to_all(value, "expert", 0, 0, tiled=True)


def local(
    tokens,
    w_query,
    w_key,
    w_value,
    w_out,
    w_router,
    gain_attn,
    gain_moe,
    w_gate,
    w_up,
    w_down,
    routes,
    seq_split,
    cotangent,
):
    z = lax.axis_index("wshard")
    me = lax.axis_index("expert")
    core = me % 2
    place = jnp.stack([z, core]).astype(jnp.int32)
    w_gate, w_up, w_down = w_gate[0], w_up[0], w_down[0]

    routes_t = routes.T
    pick_t, ups_send = call(
        routing_kernel,
        "routing",
        [((SLOTS, ROWS), bf16), ((SLOTS, WIDTH + EXTRA), bf16)],
        (routes_t, cotangent),
        4,
        vmem=ALL_VMEM,
    )
    ups = to_owners(ups_send.reshape(OWNERS, CAP, WIDTH + EXTRA)).reshape(SLOTS, WIDTH + EXTRA)
    pick, mask = call(
        mask_kernel, "mask", [((ROWS, SLOTS), bf16), ((ROWS, EXTRA), f32)], (routes,), 3
    )

    split_at = seq_split[0]
    places = jnp.arange(GROUP, dtype=jnp.int32)
    position = jnp.where(places >= split_at, places - split_at, places).astype(f32)
    exponent = jnp.arange(32, dtype=f32) * (2.0 / 64)
    angles = position[:, None] * jnp.power(rope_base, -exponent)[None, :]
    cosine, sine = jnp.cos(angles), jnp.sin(angles)
    cosine = jnp.concatenate([cosine] * 4, axis=1)
    sine = jnp.concatenate([-sine, sine] * 2, axis=1)

    gains = jnp.pad(jnp.stack([gain_attn, gain_moe]), ((0, 14), (0, 0)))
    w_own, *w_sent = call(
        pack_kernel,
        "pack",
        [((256, 640), bf16)] + [((128, 640), bf16)] * 3,
        (place, w_query, w_key, w_value, w_router, gains),
        1,
        smem=1,
        after=(pick_t,),
    )
    w_mine = call(
        stack_kernel,
        "stack",
        [((3, 128, 640), bf16)],
        z_shifts(w_sent),
        1,
        after=(cosine, sine),
    )[0]
    w_other = other_core(w_mine)
    tokens_held = call(
        hold_kernel, "hold", [((ROWS, WIDTH), bf16)], (tokens,), 1, after=(w_sent[0],)
    )[0]
    x_pieces = [tokens] + z_shifts([tokens_held] * 3)
    out_half = lax.dynamic_slice(w_out, (core * 128, 0), (128, WIDTH))
    out_halves = z_shifts([out_half] * 3)
    x_all, factor_all = call(
        norm_kernel,
        "norm",
        [((GROUP, WIDTH), bf16), ((GROUP, EXTRA), f32)],
        (place, *x_pieces),
        2,
        smem=1,
    )

    w_all, normed, query, key, value, mixed, *mixed_sent = call(
        front_kernel,
        "attention",
        [
            ((WIDTH, 640), bf16),
            ((GROUP, WIDTH), bf16),
            ((GROUP, 256), bf16),
            ((GROUP, 128), bf16),
            ((GROUP, 128), bf16),
            ((GROUP, 256), bf16),
        ]
        + [((ROWS, 256), bf16)] * 4,
        (seq_split, place, x_all, factor_all, w_own, w_mine, w_other, cosine, sine),
        8,
        smem=2,
    )
    small_all = w_all[:, 512:]
    out_mine = call(
        stack_kernel, "stack", [((3, 128, WIDTH), bf16)], out_halves, 1, after=(mixed,)
    )[0]
    out_other = other_core(out_mine)
    middle, second, gate, rows_send, out_all = call(
        middle_kernel,
        "middle",
        [
            ((ROWS, WIDTH), f32),
            ((ROWS, WIDTH), bf16),
            ((ROWS, EXTRA), f32),
            ((SLOTS, WIDTH), bf16),
            ((WIDTH, WIDTH), bf16),
        ],
        (
            place,
            mixed_sent[0],
            *z_shifts(mixed_sent[1:]),
            w_out,
            out_mine,
            out_other,
            tokens,
            small_all,
            mask,
            pick_t,
        ),
        6,
        vmem=ALL_VMEM,
        smem=1,
        scratch=[pltpu.VMEM((ROWS, WIDTH), bf16)],
    )
    rows_in = to_owners(rows_send.reshape(OWNERS, CAP, WIDTH)).reshape(SLOTS, WIDTH)
    mixed_pieces = [mixed] + z_shifts([mixed] * 3)

    weights = call(gate_kernel, "gates", [((ROWS, SLOTS), bf16)], (gate, pick), 1)[0]

    up_rows = ups[:, :WIDTH]
    h_up = (residual_scale * nt(up_rows, w_down)).astype(bf16)
    g_rows, hidden, g_gate, g_up = expert_call(rows_in, h_up, w_gate, w_up, mixed_pieces)
    back = to_owners(g_rows)

    row_gate = call(
        row_gate_kernel,
        "row_gates",
        [((SLOTS, EXTRA), f32)],
        (me.reshape(1), rows_in, ups[:, WIDTH:], small_all),
        4,
        smem=1,
        after=(hidden,),
    )[0][:, :1]
    g_out = (residual_scale * row_gate * up_rows.astype(f32)).astype(bf16)
    gate_grad = tn(rows_in, (row_gate * g_gate.astype(f32)).astype(bf16)).astype(bf16)
    up_grad = tn(rows_in, (row_gate * g_up.astype(f32)).astype(bf16)).astype(bf16)
    down_grad = tn(hidden, g_out).astype(bf16)

    def shared_sum(grad):
        parts = grad.reshape(LANES, -1, grad.shape[1])

        def part(d):
            return lax.dynamic_index_in_dim(parts, (z + d) % LANES, 0, keepdims=False)

        total = part(0).astype(f32)
        for piece in z_shifts([part(d) for d in (1, 2, 3)]):
            total += piece.astype(f32)
        return total

    gate_share, up_share, down_share = (shared_sum(g) for g in (gate_grad, up_grad, down_grad))
    expert_out = nn(hidden, w_down).astype(bf16)
    out_back = to_owners(expert_out.reshape(OWNERS, CAP, WIDTH))

    g_middle, small_grad, *branch_sent = call(
        return_kernel,
        "return",
        [((ROWS, WIDTH), f32), ((WIDTH, EXTRA), f32)] + [((ROWS, 512), bf16)] * 4,
        (place, back, pick, weights, middle, second, gate, cotangent, small_all, out_all),
        7,
        smem=1,
        scratch=[pltpu.VMEM((ROWS, WIDTH), bf16), pltpu.VMEM((ROWS, WIDTH), bf16)],
        after=(gate_share, up_share, down_share),
    )
    wide = 768 + EXTRA
    keep, give, *normed_sent = call(
        back_kernel,
        "attention_back",
        [((512, wide), bf16)] * 2 + [((ROWS, WIDTH), bf16)] * 4,
        (
            seq_split,
            place,
            branch_sent[0],
            *z_shifts(branch_sent[1:]),
            *mixed_pieces,
            query,
            key,
            value,
            normed,
            x_all,
            w_all,
            cosine,
            sine,
            small_grad,
        ),
        18,
        vmem=ALL_VMEM,
        smem=2,
        scratch=[
            pltpu.VMEM((WIDTH, wide), bf16),
            pltpu.VMEM((GROUP, WIDTH), bf16),
            pltpu.VMEM((GROUP, 256), bf16),
            pltpu.VMEM((GROUP, 256), bf16),
            pltpu.VMEM((GROUP, 256), f32),
            pltpu.VMEM((2, GROUP, 128), f32),
            pltpu.VMEM((2, GROUP, 128), f32),
        ],
    )

    output = middle + residual_scale * nn(weights, out_back.reshape(SLOTS, WIDTH))

    g_own = normed_sent[0].astype(f32)
    for piece in z_shifts(normed_sent[1:]):
        g_own += piece.astype(f32)
    x = tokens.astype(f32)
    factor = lax.rsqrt(jnp.mean(x * x, axis=-1, keepdims=True) + epsilon)
    y = x * factor
    t = g_own * small_all[:, OWNERS].astype(f32)[None, :]
    input_grad = g_middle + factor * (t - y * jnp.mean(t * y, axis=-1, keepdims=True))

    chip = call(
        add_kernel, "add", [((512, wide), bf16)], (keep, other_core(give)), 1, after=(out_back,)
    )[0]
    groups = [
        [(2 * xy + c) * LANES + a for a in range(LANES) for xy in range(OWNERS // 2)]
        for c in range(2)
    ]
    arrived = lax.all_to_all(
        chip.reshape(64, 8, wide),
        ("expert", "wshard"),
        0,
        0,
        tiled=True,
        axis_index_groups=groups,
    )
    strips = call(
        strip_kernel,
        "strip",
        [((128, 3072 + EXTRA), bf16)],
        (arrived.reshape(512, wide),),
        2,
        after=(output, input_grad),
    )[0]
    shared = lax.all_to_all(
        strips.reshape(OWNERS // 2, 8, 3072 + EXTRA),
        "expert",
        0,
        0,
        tiled=True,
        axis_index_groups=[[2 * xy + c for xy in range(OWNERS // 2)] for c in range(2)],
    ).reshape(128, 3072 + EXTRA)
    dense = final_call(0, place, shared, ())
    dense = final_call(1, place, other_core(shared), dense)
    grad_query, grad_key, grad_value, grad_out, grad_router, grad_gain_m, grad_gain_a = dense

    return (
        output,
        input_grad,
        grad_query,
        grad_key,
        grad_value,
        grad_out,
        grad_router,
        grad_gain_a[0],
        grad_gain_m[0],
        gate_share[None],
        up_share[None],
        down_share[None],
    )


def solution(mesh):
    rows = P(("expert", "wshard"), None)
    dense = P("wshard", None)
    expert = P("expert", None, None)
    shard = P("expert", "wshard", None)
    in_specs = (rows,) + (dense,) * 5 + (P("wshard"),) * 2 + (expert,) * 3
    in_specs += (rows, P("expert"), rows)
    out_specs = (rows, rows) + (dense,) * 5 + (P("wshard"),) * 2 + (shard,) * 3
    return jax.shard_map(local, mesh=mesh, in_specs=in_specs, out_specs=out_specs, check_vma=False)
```

```python
import functools

import jax
import jax.numpy as jnp
from jax import lax
from jax.experimental import pallas as pl
from jax.experimental.pallas import tpu as pltpu
from jax.sharding import PartitionSpec as P

f32 = jnp.float32
bf16 = jnp.bfloat16
epsilon = 1e-06
residual_scale = 0.22
score_scale = 0.015625
rope_base = 10000.0

LANES = 4
OWNERS = 32
ROWS = 192
GROUP = 768
WIDTH = 1024
CAP = 64
SLOTS = OWNERS * CAP
FF = 512
TOP = 8
EXTRA = 128
VMEM = 50 * 1024 * 1024
ALL_VMEM = 60 * 1024 * 1024


def nn(a, b):
    return lax.dot_general(a, b, (((1,), (0,)), ((), ())), preferred_element_type=f32)


def nt(a, b):
    return lax.dot_general(a, b, (((1,), (1,)), ((), ())), preferred_element_type=f32)


def tn(a, b):
    return lax.dot_general(a, b, (((0,), (0,)), ((), ())), preferred_element_type=f32)


def iota(shape, axis):
    return lax.broadcasted_iota(jnp.int32, shape, axis)


def split_two(v):
    high = v.astype(bf16)
    return high, (v - high.astype(f32)).astype(bf16)


def cost(us):
    return pl.CostEstimate(
        flops=int(us * 1e9), bytes_accessed=int(us * 3.5e6), transcendentals=0
    )


def call(kernel, name, outs, args, us, smem=0, scratch=(), after=(), vmem=VMEM):
    specs = [pl.BlockSpec(memory_space=pltpu.SMEM)] * smem
    specs += [pl.BlockSpec(memory_space=pltpu.VMEM)] * (len(args) - smem)
    specs += [pl.BlockSpec(memory_space=pltpu.HBM)] * len(after)
    first, last = len(args), len(args) + len(after)
    args = tuple(args) + tuple(after)
    body = kernel

    def kernel(*refs):
        body(*refs[:first], *refs[last:])
    return pl.pallas_call(
        kernel,
        name=name,
        out_shape=[jax.ShapeDtypeStruct(s, d) for s, d in outs],
        in_specs=specs,
        out_specs=[pl.BlockSpec(memory_space=pltpu.VMEM)] * len(outs),
        scratch_shapes=list(scratch),
        cost_estimate=cost(us),
        compiler_params=pltpu.CompilerParams(vmem_limit_bytes=vmem),
    )(*args)


def spread_rows():
    same = (iota((SLOTS, EXTRA), 0) // CAP) == iota((SLOTS, EXTRA), 1)
    return same.astype(f32).astype(bf16)


def earlier():
    return (iota((ROWS, ROWS), 0) < iota((ROWS, ROWS), 1)).astype(f32).astype(bf16)


def routing_kernel(routes_t, cot, pick_t, rows_out):
    sub = iota((EXTRA, ROWS), 0)
    mask_t = jnp.zeros((EXTRA, ROWS), f32)
    for k in range(TOP):
        mask_t += (routes_t[k : k + 1, :] == sub).astype(f32)
    mask_tb = mask_t.astype(bf16)
    before_t = nn(mask_tb, earlier())
    slot = iota((CAP, ROWS), 0).astype(f32)
    p_t = jnp.concatenate(
        [
            jnp.where(before_t[e : e + 1] == slot, mask_t[e : e + 1], 0.0).astype(bf16)
            for e in range(OWNERS)
        ],
        axis=0,
    )
    pick_t[...] = p_t
    rows_out[:, :WIDTH] = nn(p_t, cot[...]).astype(bf16)
    rows_out[:, WIDTH:] = nt(p_t, mask_tb).astype(bf16)


def mask_kernel(routes, pick, mask_out):
    lane = iota((ROWS, EXTRA), 1)
    mask = jnp.zeros((ROWS, EXTRA), f32)
    for k in range(TOP):
        mask += (routes[:, k : k + 1] == lane).astype(f32)
    mask_out[...] = mask
    mask_b = mask.astype(bf16)
    before = tn(earlier(), mask_b).astype(bf16)
    spread = spread_rows()
    slot = (iota((ROWS, SLOTS), 1) % CAP).astype(f32)
    pick[...] = jnp.where(nt(before, spread) == slot, nt(mask_b, spread), 0.0).astype(bf16)


def gate_kernel(gate, pick, weights):
    spread = spread_rows()
    high, low = split_two(gate[...])
    w = pick[...].astype(f32) * (nt(high, spread) + nt(low, spread))
    weights[...] = w.astype(bf16)


def swap_halves(t):
    lane = iota(t.shape, 1) % 64
    return jnp.where(lane < 32, pltpu.roll(t, 96, 1), pltpu.roll(t, 32, 1))


def allowed(split, low, rows, keys):
    qi = iota((rows, keys), 0) + low
    kj = iota((rows, keys), 1)
    start = jnp.where(qi >= split, split, 0)
    return (kj <= qi) & (kj >= start)


BLOCK = 256
BLOCKS = GROUP // BLOCK


def head_place(h):
    return h // 2, h % 2, (h // 2) != (h % 2)


def source(z, d):
    return (z + LANES - d) % LANES


def rows_at(start, size, step):
    return pl.ds(pl.multiple_of(start, step), size)


def pack_kernel(
    place, w_query, w_key, w_value, w_router, gains, w_out, own, out_half, *sent
):
    z, core = place[0], place[1]
    select = ((iota((16, EXTRA), 1) - OWNERS) == iota((16, EXTRA), 0)) & (iota((16, EXTRA), 0) < 2)
    small = tn(gains[...], select.astype(f32).astype(bf16)).astype(bf16)
    own[:, 512:640] = small
    own[:, 512 : 512 + OWNERS] = w_router[...]

    def fill(out, dest, rows):
        out[:, :256] = w_query[rows, rows_at(dest * 256, 256, 256)]
        out[:, 256:384] = w_key[rows, rows_at(dest * 128, 128, 128)]
        out[:, 384:512] = w_value[rows, rows_at(dest * 128, 128, 128)]

    fill(own, z, slice(None))
    half = rows_at(core * 128, 128, 128)
    out_half[...] = w_out[half, :]
    for d, out in enumerate(sent):
        fill(out, (z + d + 1) % LANES, half)
        out[:, 512:640] = own[half, 512:640]


def norm_kernel(place, x0, x1, x2, x3, x_ref, factor):
    for d, piece in enumerate((x0, x1, x2, x3)):
        x_ref[rows_at(source(place[0], d) * ROWS, ROWS, 64), :] = piece[...]
    x = x_ref[...].astype(f32)
    r = lax.rsqrt(jnp.mean(x * x, axis=-1, keepdims=True) + epsilon)
    factor[...] = jnp.broadcast_to(r, (GROUP, EXTRA))


def gain_row(small, which):
    select = (iota((16, EXTRA), 1) == OWNERS + which).astype(f32).astype(bf16)
    return nt(select, small)[:1]


def front_kernel(
    split,
    place,
    x_ref,
    factor,
    w_own,
    w_mine,
    w_other,
    cosine,
    sine,
    w_ref,
    normed,
    q_out,
    k_out,
    v_out,
    mixed,
    m0,
    m1,
    m2,
    m3,
):
    z, core = place[0], place[1]
    w_ref[rows_at(z * 256, 256, 256), :] = w_own[...]
    for d in (1, 2, 3):
        start = source(z, d) * 256
        w_ref[rows_at(start + core * 128, 128, 128), :] = w_mine[d - 1]
        w_ref[rows_at(start + (1 - core) * 128, 128, 128), :] = w_other[d - 1]
    x = x_ref[...].astype(f32)
    normed_b = (x * factor[:, :1] * gain_row(w_ref[:, 512:640], 0)).astype(bf16)
    normed[...] = normed_b
    lin = nn(normed_b, w_ref[:, :512])
    c, s = cosine[...], sine[...]
    for g in range(2):
        part = lin[:, 128 * g : 128 * g + 128]
        q_out[:, 128 * g : 128 * g + 128] = (part * c + swap_halves(part) * s).astype(bf16)
    part = lin[:, 256:384]
    key = part * c + swap_halves(part) * s
    key_b = key.astype(bf16)
    k_out[...] = key_b
    value_b = lin[:, 384:512].astype(bf16)
    v_out[...] = value_b
    keys = (key_b, pltpu.roll(key_b.astype(f32), 64, 1).astype(bf16))
    values = (value_b, pltpu.roll(value_b.astype(f32), 64, 1).astype(bf16))
    low_half = iota((BLOCK, 128), 1) < 64
    for i in range(BLOCKS):
        n = (i + 1) * BLOCK
        ok = allowed(split[0], i * BLOCK, BLOCK, n)
        for g in range(2):
            q2 = q_out[i * BLOCK : (i + 1) * BLOCK, 128 * g : 128 * g + 128].astype(f32) * score_scale
            halves = []
            for half in range(2):
                turned = g != half
                mine = low_half if half == 0 else ~low_half
                qh = jnp.where(mine, q2, 0.0).astype(bf16)
                scores = jnp.where(ok, nt(qh, keys[turned][:n]), -1e30)
                top = jnp.max(scores, axis=-1, keepdims=True)
                e = jnp.exp(scores - top)
                share = 1.0 / jnp.sum(e, axis=-1, keepdims=True)
                halves.append(share * nn(e.astype(bf16), values[turned][:n]))
            mixed[i * BLOCK : (i + 1) * BLOCK, 128 * g : 128 * g + 128] = jnp.where(
                low_half, halves[0], halves[1]
            ).astype(bf16)
    for d, out in enumerate((m0, m1, m2, m3)):
        out[...] = mixed[rows_at(((z + d) % LANES) * ROWS, ROWS, 64), :]


def middle_kernel(
    place,
    m0,
    m1,
    m2,
    m3,
    out_own,
    out_mine,
    out_other,
    x_ref,
    router,
    mask,
    pick_t,
    middle,
    second,
    gate,
    rows_out,
    w_out,
    mixed,
):
    z, core = place[0], place[1]
    for d, piece in enumerate((m0, m1, m2, m3)):
        mixed[:, rows_at(source(z, d) * 256, 256, 256)] = piece[...]
    w_out[rows_at(z * 256, 256, 256), :] = out_own[...]
    for d in (1, 2, 3):
        start = source(z, d) * 256
        w_out[rows_at(start + core * 128, 128, 128), :] = out_mine[d - 1]
        w_out[rows_at(start + (1 - core) * 128, 128, 128), :] = out_other[d - 1]
    mid = x_ref[...].astype(f32) + residual_scale * nn(mixed[...], w_out[...])
    middle[...] = mid
    factor = lax.rsqrt(jnp.mean(mid * mid, axis=-1, keepdims=True) + epsilon)
    second_b = (mid * factor * gain_row(router[...], 1)).astype(bf16)
    second[...] = second_b
    chosen = mask[...] > 0.5
    logits = jnp.where(chosen, nn(second_b, router[...]), -1e30)
    top = jnp.max(logits, axis=-1, keepdims=True)
    e = jnp.where(chosen, jnp.exp(logits - top), 0.0)
    gate[...] = e / jnp.sum(e, axis=-1, keepdims=True)
    rows_out[...] = nn(pick_t[...], second_b).astype(bf16)


EXPERT_BLOCK = 512
PARTS = WIDTH // 128
PACKED = PARTS * CAP + 16


def expert_kernel(rows, h_up, w_gate, w_up, *rest):
    g_rows, hidden, g_gate, g_up = rest[-4:]
    r = rows[...]
    gate_lin = nn(r, w_gate[...])
    up_lin = nn(r, w_up[...])
    sig = 1.0 / (1.0 + jnp.exp(-gate_lin))
    act = gate_lin * sig
    hidden_b = (act * up_lin).astype(bf16)
    hidden[...] = hidden_b
    g_hidden = h_up[...].astype(f32)
    g = jnp.sum(hidden_b.astype(f32) * g_hidden, axis=-1, keepdims=True)
    gg = (g_hidden * up_lin * (sig * (1.0 + gate_lin * (1.0 - sig)))).astype(bf16)
    gu = (g_hidden * act).astype(bf16)
    g_gate[...] = gg
    g_up[...] = gu
    result = (nt(gg, w_gate[...]) + nt(gu, w_up[...])).astype(bf16)
    lane, slot = iota((CAP, 128), 1), iota((CAP, 128), 0)
    high = g.astype(bf16).astype(f32)
    for s in range(EXPERT_BLOCK // CAP):
        here = slice(CAP * s, CAP * s + CAP)
        for j in range(PARTS):
            g_rows[s, CAP * j : CAP * j + CAP, :] = result[here, 128 * j : 128 * j + 128]
        spread = jnp.where(
            lane == slot,
            high[here],
            jnp.where(lane == slot + CAP, (g - high)[here], 0.0),
        )
        scalars = jnp.sum(spread, axis=0, keepdims=True)
        g_rows[s, PARTS * CAP :, :] = jnp.broadcast_to(scalars, (16, 128)).astype(bf16)


def row_gate_kernel(me, rows, mask, router, out):
    chosen = mask[...].astype(f32) > 0.5
    logits = jnp.where(chosen, nn(rows[...], router[...]), -1e30)
    top = jnp.max(logits, axis=-1, keepdims=True)
    e = jnp.where(chosen, jnp.exp(logits - top), 0.0)
    total = jnp.sum(e, axis=-1, keepdims=True)
    mine = jnp.sum(jnp.where(iota((SLOTS, EXTRA), 1) == me[0], e, 0.0), axis=-1, keepdims=True)
    out[...] = jnp.broadcast_to(mine / jnp.where(total > 0, total, 1.0), (SLOTS, EXTRA))


def hold_kernel(value, out):
    out[...] = value[...]


def stack_kernel(a, b, c, out):
    out[0], out[1], out[2] = a[...], b[...], c[...]


def expert_call(rows, h_up, w_gate, w_up, after):
    def whole(shape):
        return pl.BlockSpec(shape, lambda i: (0, 0))

    def blocked(width):
        return pl.BlockSpec((EXPERT_BLOCK, width), lambda i: (i, 0))

    return pl.pallas_call(
        expert_kernel,
        name="expert",
        grid=(SLOTS // EXPERT_BLOCK,),
        out_shape=[jax.ShapeDtypeStruct((OWNERS, PACKED, 128), bf16)]
        + [jax.ShapeDtypeStruct((SLOTS, FF), bf16)] * 3,
        in_specs=[blocked(WIDTH), blocked(FF), whole((WIDTH, FF)), whole((WIDTH, FF))]
        + [pl.BlockSpec(memory_space=pltpu.HBM)] * len(after),
        out_specs=[pl.BlockSpec((EXPERT_BLOCK // CAP, PACKED, 128), lambda i: (i, 0, 0))]
        + [blocked(FF)] * 3,
        cost_estimate=cost(15),
        compiler_params=pltpu.CompilerParams(vmem_limit_bytes=60 * 1024 * 1024),
    )(rows, h_up, w_gate, w_up, *after)


def return_kernel(
    place,
    back,
    pick,
    weights,
    middle,
    second,
    gate,
    cot,
    router,
    w_out,
    g_middle_out,
    small_out,
    p0,
    p1,
    p2,
    p3,
    g_branch,
    g_mixed,
):
    lane = iota((ROWS, EXTRA), 1)
    spread = spread_rows()
    scalars = nn(spread[:, :OWNERS], back[:, PARTS * CAP, :])
    offset, lanes = iota((SLOTS, EXTRA), 0) % CAP, iota((SLOTS, EXTRA), 1)
    column = jnp.sum(jnp.where(lanes % CAP == offset, scalars, 0.0), axis=-1, keepdims=True)
    high, low = split_two(spread.astype(f32) * column)
    g_gate = nn(pick[...], high) + nn(pick[...], low)
    probs = gate[...]
    g_logits = probs * (g_gate - jnp.sum(probs * g_gate, axis=-1, keepdims=True))
    high, low = split_two(g_logits)
    w = router[...]
    pieces = [
        back[:, CAP * j : CAP * j + CAP, :].reshape(SLOTS, 128) for j in range(PARTS)
    ]
    summed = [
        nn(weights[...], jnp.concatenate(pieces[j : j + 2], axis=1)) for j in range(0, PARTS, 2)
    ]
    g_second = jnp.concatenate(summed, axis=1) + (nt(high, w) + nt(low, w))
    mid = middle[...]
    factor = lax.rsqrt(jnp.mean(mid * mid, axis=-1, keepdims=True) + epsilon)
    z = mid * factor
    t = g_second * gain_row(w, 1)
    g_middle = cot[...].astype(f32) + factor * (t - z * jnp.mean(t * z, axis=-1, keepdims=True))
    g_middle_out[...] = g_middle
    branch_b = (residual_scale * g_middle).astype(bf16)
    g_branch[...] = branch_b
    g_mixed[...] = nt(branch_b, w_out[...]).astype(bf16)
    for d, out in enumerate((p0, p1, p2, p3)):
        there = rows_at(((place[0] + d) % LANES) * 256, 256, 256)
        out[:, :256] = g_mixed[:, there]
        out[:, 256:] = g_branch[:, there]
    s = second[...]
    one = (lane == OWNERS).astype(f32).astype(bf16)
    ph, plow = split_two(g_second * z)
    small_out[...] = tn(s, high) + tn(s, low) + tn(ph, one) + tn(plow, one)


def back_kernel(
    split,
    place,
    p0,
    p1,
    p2,
    p3,
    m0,
    m1,
    m2,
    m3,
    q_ref,
    k_ref,
    v_ref,
    normed,
    x_ref,
    w_ref,
    cosine,
    sine,
    small_in,
    keep,
    give,
    n0,
    n1,
    n2,
    n3,
    grads,
    g_normed_out,
    g_mixed,
    g_branch,
    g_query,
    g_key,
    g_value,
):
    z, core = place[0], place[1]
    for d, piece in enumerate((p0, p1, p2, p3)):
        rows = rows_at(source(z, d) * ROWS, ROWS, 64)
        g_mixed[rows, :] = piece[:, :256]
        g_branch[rows, :] = piece[:, 256:]
    key_b, value_b = k_ref[...], v_ref[...]
    keys = (key_b, pltpu.roll(key_b.astype(f32), 64, 1).astype(bf16))
    values = (value_b, pltpu.roll(value_b.astype(f32), 64, 1).astype(bf16))
    g_key[...] = jnp.zeros_like(g_key)
    g_value[...] = jnp.zeros_like(g_value)
    low_half = iota((BLOCK, 128), 1) < 64
    for i in range(BLOCKS):
        n = (i + 1) * BLOCK
        here = slice(i * BLOCK, (i + 1) * BLOCK)
        ok = allowed(split[0], i * BLOCK, BLOCK, n)
        for g in range(2):
            q2 = q_ref[here, 128 * g : 128 * g + 128].astype(f32) * score_scale
            gm2 = g_mixed[here, 128 * g : 128 * g + 128].astype(f32)
            halves = []
            for half in range(2):
                turned = int(g != half)
                mine = low_half if half == 0 else ~low_half
                qh = jnp.where(mine, q2, 0.0).astype(bf16)
                gm = jnp.where(mine, gm2, 0.0).astype(bf16)
                scores = jnp.where(ok, nt(qh, keys[turned][:n]), -1e30)
                top = jnp.max(scores, axis=-1, keepdims=True)
                e = jnp.exp(scores - top)
                share = 1.0 / jnp.sum(e, axis=-1, keepdims=True)
                gp = nt(gm, values[turned][:n])
                mean = share * jnp.sum(e * gp, axis=-1, keepdims=True)
                gs = (e * (gp - mean)).astype(bf16)
                halves.append(share * nn(gs, keys[turned][:n]))
                g_key[turned, :n, :] += tn(gs, (share * qh.astype(f32)).astype(bf16))
                g_value[turned, :n, :] += tn(e.astype(bf16), (share * gm.astype(f32)).astype(bf16))
            g_query[here, 128 * g : 128 * g + 128] = score_scale * jnp.where(
                low_half, halves[0], halves[1]
            )
    c, s = cosine[...], sine[...]

    def unturn(t):
        return (t * c - swap_halves(t) * s).astype(bf16)

    g_lin = jnp.concatenate(
        [
            unturn(g_query[:, :128]),
            unturn(g_query[:, 128:]),
            unturn(g_key[0] + pltpu.roll(g_key[1], 64, 1)),
            (g_value[0] + pltpu.roll(g_value[1], 64, 1)).astype(bf16),
        ],
        axis=1,
    )
    grads[:, :512] = tn(normed[...], g_lin).astype(bf16)
    for d, piece in enumerate((m0, m1, m2, m3)):
        grads[rows_at(source(z, d) * 256, 256, 256), 512:768] = tn(piece[...], g_branch[...]).astype(bf16)
    g_normed = nt(g_lin, w_ref[:, :512])
    g_normed_out[...] = g_normed.astype(bf16)
    x = x_ref[...].astype(f32)
    y = x * lax.rsqrt(jnp.mean(x * x, axis=-1, keepdims=True) + epsilon)
    one = (iota((GROUP, EXTRA), 1) == OWNERS + 1).astype(f32).astype(bf16)
    ph, plow = split_two(g_normed * y)
    grads[:, 768:] = (small_in[...] + tn(ph, one) + tn(plow, one)).astype(bf16)
    for a in range(LANES):
        keep[128 * a : 128 * a + 128, :] = grads[rows_at(a * 256 + core * 128, 128, 128), :]
        give[128 * a : 128 * a + 128, :] = grads[rows_at(a * 256 + (1 - core) * 128, 128, 128), :]
    for d, out in enumerate((n0, n1, n2, n3)):
        out[...] = g_normed_out[rows_at(((z + d) % LANES) * ROWS, ROWS, 64), :]


def add_kernel(a, b, out):
    out[...] = (a[...].astype(f32) + b[...].astype(f32)).astype(bf16)


def strip_kernel(arrived, out):
    total = jnp.sum(arrived[...].astype(f32).reshape(LANES, 16, 8, 768 + EXTRA), axis=1)
    parts = [total[a, :, :256] for a in range(LANES)]
    parts += [total[a, :, 256:384] for a in range(LANES)]
    parts += [total[a, :, 384:512] for a in range(LANES)]
    parts += [total[a, :, 512:768] for a in range(LANES)]
    strip = jnp.concatenate(parts + [jnp.sum(total[:, :, 768:], axis=0)], axis=1)
    out[...] = jnp.concatenate([strip] * 16, axis=0).astype(bf16)


def final_kernel(place, piece, *refs):
    query, key, value, out, router, gain_m, gain_a = refs[-7:]
    query[...] = piece[:, :1024].astype(f32)
    key[...] = piece[:, 1024:1536].astype(f32)
    value[...] = piece[:, 1536:2048].astype(f32)
    out[...] = piece[:, 2048:3072].astype(f32)
    select = iota((64, EXTRA), 1) == iota((64, EXTRA), 0)
    small = nt(select.astype(f32).astype(bf16), piece[:, 3072:])
    router[...] = small[:OWNERS]
    gain_m[...] = small[OWNERS : OWNERS + 1]
    gain_a[...] = small[OWNERS + 1 : OWNERS + 2]


def final_call(half, place, piece, before):
    def rows(width):
        return pl.BlockSpec((128, width), lambda i, p: ((p[1] + half) % 2, 0))

    def columns(height):
        return pl.BlockSpec((height, 128), lambda i, p: (0, (p[1] + half) % 2))

    widths, heights = (1024, 512, 512, 1024), (OWNERS, 1, 1)
    shapes = [(256, w) for w in widths] + [(h, 256) for h in heights]
    return pl.pallas_call(
        final_kernel,
        name="final",
        out_shape=[jax.ShapeDtypeStruct(s, f32) for s in shapes],
        grid_spec=pltpu.PrefetchScalarGridSpec(
            num_scalar_prefetch=1,
            grid=(1,),
            in_specs=[pl.BlockSpec((128, 3072 + EXTRA), lambda i, p: (0, 0))]
            + [pl.BlockSpec(memory_space=pltpu.HBM)] * len(before),
            out_specs=[rows(w) for w in widths] + [columns(h) for h in heights],
        ),
        input_output_aliases={2 + i: i for i in range(len(before))},
        cost_estimate=cost(1),
        compiler_params=pltpu.CompilerParams(vmem_limit_bytes=VMEM),
    )(place, piece, *before)


def z_shift(value, d):
    return lax.ppermute(value, "wshard", [(i, (i + d) % LANES) for i in range(LANES)])


def z_shifts(values):
    return [z_shift(v, d) for d, v in zip((1, 2, 3), values)]


def other_core(value):
    return lax.ppermute(value, "expert", [(i, i ^ 1) for i in range(OWNERS)])


def to_owners(value):
    return lax.all_to_all(value, "expert", 0, 0, tiled=True)


def local(
    tokens,
    w_query,
    w_key,
    w_value,
    w_out,
    w_router,
    gain_attn,
    gain_moe,
    w_gate,
    w_up,
    w_down,
    routes,
    seq_split,
    cotangent,
):
    z = lax.axis_index("wshard")
    me = lax.axis_index("expert")
    core = me % 2
    place = jnp.stack([z, core]).astype(jnp.int32)
    w_gate, w_up, w_down = w_gate[0], w_up[0], w_down[0]

    routes_t = routes.T
    pick_t, ups_send = call(
        routing_kernel,
        "routing",
        [((SLOTS, ROWS), bf16), ((SLOTS, WIDTH + EXTRA), bf16)],
        (routes_t, cotangent),
        4,
        vmem=ALL_VMEM,
    )
    ups = to_owners(ups_send.reshape(OWNERS, CAP, WIDTH + EXTRA)).reshape(SLOTS, WIDTH + EXTRA)
    pick, mask = call(
        mask_kernel, "mask", [((ROWS, SLOTS), bf16), ((ROWS, EXTRA), f32)], (routes,), 3
    )

    split_at = seq_split[0]
    places = jnp.arange(GROUP, dtype=jnp.int32)
    position = jnp.where(places >= split_at, places - split_at, places).astype(f32)
    exponent = jnp.arange(32, dtype=f32) * (2.0 / 64)
    angles = position[:, None] * jnp.power(rope_base, -exponent)[None, :]
    cosine, sine = jnp.cos(angles), jnp.sin(angles)
    cosine = jnp.concatenate([cosine] * 4, axis=1)
    sine = jnp.concatenate([-sine, sine] * 2, axis=1)

    gains = jnp.pad(jnp.stack([gain_attn, gain_moe]), ((0, 14), (0, 0)))
    w_own, out_half, *w_sent = call(
        pack_kernel,
        "pack",
        [((256, 640), bf16), ((128, WIDTH), bf16)] + [((128, 640), bf16)] * 3,
        (place, w_query, w_key, w_value, w_router, gains, w_out),
        1,
        smem=1,
        after=(pick_t,),
    )
    w_pieces = z_shifts(w_sent)
    w_mine = call(
        stack_kernel, "stack", [((3, 128, 640), bf16)], w_pieces, 1, after=(cosine, sine)
    )[0]
    w_other = other_core(w_mine)
    tokens_held = call(
        hold_kernel, "hold", [((ROWS, WIDTH), bf16)], (tokens,), 1, after=(w_pieces[0],)
    )[0]
    x_pieces = [tokens] + z_shifts([tokens_held] * 3)
    out_halves = z_shifts([out_half] * 3)
    x_all, factor_all = call(
        norm_kernel,
        "norm",
        [((GROUP, WIDTH), bf16), ((GROUP, EXTRA), f32)],
        (place, *x_pieces),
        2,
        smem=1,
    )

    w_all, normed, query, key, value, mixed, *mixed_sent = call(
        front_kernel,
        "attention",
        [
            ((WIDTH, 640), bf16),
            ((GROUP, WIDTH), bf16),
            ((GROUP, 256), bf16),
            ((GROUP, 128), bf16),
            ((GROUP, 128), bf16),
            ((GROUP, 256), bf16),
        ]
        + [((ROWS, 256), bf16)] * 4,
        (seq_split, place, x_all, factor_all, w_own, w_mine, w_other, cosine, sine),
        8,
        smem=2,
    )
    small_all = w_all[:, 512:]
    out_mine = call(
        stack_kernel, "stack", [((3, 128, WIDTH), bf16)], out_halves, 1, after=(mixed,)
    )[0]
    out_other = other_core(out_mine)
    middle, second, gate, rows_send, out_all = call(
        middle_kernel,
        "middle",
        [
            ((ROWS, WIDTH), f32),
            ((ROWS, WIDTH), bf16),
            ((ROWS, EXTRA), f32),
            ((SLOTS, WIDTH), bf16),
            ((WIDTH, WIDTH), bf16),
        ],
        (
            place,
            mixed_sent[0],
            *z_shifts(mixed_sent[1:]),
            w_out,
            out_mine,
            out_other,
            tokens,
            small_all,
            mask,
            pick_t,
        ),
        6,
        vmem=ALL_VMEM,
        smem=1,
        scratch=[pltpu.VMEM((ROWS, WIDTH), bf16)],
    )
    rows_in = to_owners(rows_send.reshape(OWNERS, CAP, WIDTH)).reshape(SLOTS, WIDTH)
    mixed_pieces = [mixed] + z_shifts([mixed] * 3)

    weights = call(gate_kernel, "gates", [((ROWS, SLOTS), bf16)], (gate, pick), 1)[0]

    up_rows = ups[:, :WIDTH]
    h_up = (residual_scale * nt(up_rows, w_down)).astype(bf16)
    g_rows, hidden, g_gate, g_up = expert_call(rows_in, h_up, w_gate, w_up, mixed_pieces)
    back = to_owners(g_rows)

    row_gate = call(
        row_gate_kernel,
        "row_gates",
        [((SLOTS, EXTRA), f32)],
        (me.reshape(1), rows_in, ups[:, WIDTH:], small_all),
        4,
        smem=1,
        after=(hidden,),
    )[0][:, :1]
    g_out = (residual_scale * row_gate * up_rows.astype(f32)).astype(bf16)
    gate_grad = tn(rows_in, (row_gate * g_gate.astype(f32)).astype(bf16)).astype(bf16)
    up_grad = tn(rows_in, (row_gate * g_up.astype(f32)).astype(bf16)).astype(bf16)
    down_grad = tn(hidden, g_out).astype(bf16)

    def shared_sum(grad):
        parts = grad.reshape(LANES, -1, grad.shape[1])

        def part(d):
            return lax.dynamic_index_in_dim(parts, (z + d) % LANES, 0, keepdims=False)

        total = part(0).astype(f32)
        for piece in z_shifts([part(d) for d in (1, 2, 3)]):
            total += piece.astype(f32)
        return total

    gate_share, up_share, down_share = (shared_sum(g) for g in (gate_grad, up_grad, down_grad))
    expert_out = nn(hidden, w_down).astype(bf16)
    out_back = to_owners(expert_out.reshape(OWNERS, CAP, WIDTH))

    g_middle, small_grad, *branch_sent = call(
        return_kernel,
        "return",
        [((ROWS, WIDTH), f32), ((WIDTH, EXTRA), f32)] + [((ROWS, 512), bf16)] * 4,
        (place, back, pick, weights, middle, second, gate, cotangent, small_all, out_all),
        7,
        smem=1,
        scratch=[pltpu.VMEM((ROWS, WIDTH), bf16), pltpu.VMEM((ROWS, WIDTH), bf16)],
        after=(gate_share, up_share, down_share),
    )
    wide = 768 + EXTRA
    keep, give, *normed_sent = call(
        back_kernel,
        "attention_back",
        [((512, wide), bf16)] * 2 + [((ROWS, WIDTH), bf16)] * 4,
        (
            seq_split,
            place,
            branch_sent[0],
            *z_shifts(branch_sent[1:]),
            *mixed_pieces,
            query,
            key,
            value,
            normed,
            x_all,
            w_all,
            cosine,
            sine,
            small_grad,
        ),
        18,
        vmem=ALL_VMEM,
        smem=2,
        scratch=[
            pltpu.VMEM((WIDTH, wide), bf16),
            pltpu.VMEM((GROUP, WIDTH), bf16),
            pltpu.VMEM((GROUP, 256), bf16),
            pltpu.VMEM((GROUP, 256), bf16),
            pltpu.VMEM((GROUP, 256), f32),
            pltpu.VMEM((2, GROUP, 128), f32),
            pltpu.VMEM((2, GROUP, 128), f32),
        ],
    )

    output = middle + residual_scale * nn(weights, out_back.reshape(SLOTS, WIDTH))

    g_own = normed_sent[0].astype(f32)
    for piece in z_shifts(normed_sent[1:]):
        g_own += piece.astype(f32)
    x = tokens.astype(f32)
    factor = lax.rsqrt(jnp.mean(x * x, axis=-1, keepdims=True) + epsilon)
    y = x * factor
    t = g_own * small_all[:, OWNERS].astype(f32)[None, :]
    input_grad = g_middle + factor * (t - y * jnp.mean(t * y, axis=-1, keepdims=True))

    chip = call(
        add_kernel, "add", [((512, wide), bf16)], (keep, other_core(give)), 1, after=(out_back,)
    )[0]
    groups = [
        [(2 * xy + c) * LANES + a for a in range(LANES) for xy in range(OWNERS // 2)]
        for c in range(2)
    ]
    arrived = lax.all_to_all(
        chip.reshape(64, 8, wide),
        ("expert", "wshard"),
        0,
        0,
        tiled=True,
        axis_index_groups=groups,
    )
    strips = call(
        strip_kernel,
        "strip",
        [((128, 3072 + EXTRA), bf16)],
        (arrived.reshape(512, wide),),
        2,
        after=(output, input_grad),
    )[0]
    shared = lax.all_to_all(
        strips.reshape(OWNERS // 2, 8, 3072 + EXTRA),
        "expert",
        0,
        0,
        tiled=True,
        axis_index_groups=[[2 * xy + c for xy in range(OWNERS // 2)] for c in range(2)],
    ).reshape(128, 3072 + EXTRA)
    dense = final_call(0, place, shared, ())
    dense = final_call(1, place, other_core(shared), dense)
    grad_query, grad_key, grad_value, grad_out, grad_router, grad_gain_m, grad_gain_a = dense

    return (
        output,
        input_grad,
        grad_query,
        grad_key,
        grad_value,
        grad_out,
        grad_router.T,
        grad_gain_a[0],
        grad_gain_m[0],
        gate_share[None],
        up_share[None],
        down_share[None],
    )


def solution(mesh):
    rows = P(("expert", "wshard"), None)
    dense = P("wshard", None)
    expert = P("expert", None, None)
    shard = P("expert", "wshard", None)
    in_specs = (rows,) + (dense,) * 5 + (P("wshard"),) * 2 + (expert,) * 3
    in_specs += (rows, P("expert"), rows)
    out_specs = (rows, rows) + (dense,) * 5 + (P("wshard"),) * 2 + (shard,) * 3
    return jax.shard_map(local, mesh=mesh, in_specs=in_specs, out_specs=out_specs, check_vma=False)
```

```python
import functools

import jax
import jax.numpy as jnp
from jax import lax
from jax.experimental import pallas as pl
from jax.experimental.pallas import tpu as pltpu
from jax.sharding import PartitionSpec as P

f32 = jnp.float32
bf16 = jnp.bfloat16
epsilon = 1e-06
residual_scale = 0.22
score_scale = 0.015625
rope_base = 10000.0

LANES = 4
OWNERS = 32
ROWS = 192
GROUP = 768
WIDTH = 1024
CAP = 64
SLOTS = OWNERS * CAP
FF = 512
TOP = 8
EXTRA = 128
VMEM = 50 * 1024 * 1024
ALL_VMEM = 60 * 1024 * 1024


def nn(a, b):
    return lax.dot_general(a, b, (((1,), (0,)), ((), ())), preferred_element_type=f32)


def nt(a, b):
    return lax.dot_general(a, b, (((1,), (1,)), ((), ())), preferred_element_type=f32)


def tn(a, b):
    return lax.dot_general(a, b, (((0,), (0,)), ((), ())), preferred_element_type=f32)


def iota(shape, axis):
    return lax.broadcasted_iota(jnp.int32, shape, axis)


def split_two(v):
    high = v.astype(bf16)
    return high, (v - high.astype(f32)).astype(bf16)


def cost(us):
    return pl.CostEstimate(
        flops=int(us * 1e9), bytes_accessed=int(us * 3.5e6), transcendentals=0
    )


def call(kernel, name, outs, args, us, smem=0, scratch=(), after=(), vmem=VMEM):
    specs = [pl.BlockSpec(memory_space=pltpu.SMEM)] * smem
    specs += [pl.BlockSpec(memory_space=pltpu.VMEM)] * (len(args) - smem)
    specs += [pl.BlockSpec(memory_space=pltpu.HBM)] * len(after)
    first, last = len(args), len(args) + len(after)
    args = tuple(args) + tuple(after)
    body = kernel

    def kernel(*refs):
        body(*refs[:first], *refs[last:])
    return pl.pallas_call(
        kernel,
        name=name,
        out_shape=[jax.ShapeDtypeStruct(s, d) for s, d in outs],
        in_specs=specs,
        out_specs=[pl.BlockSpec(memory_space=pltpu.VMEM)] * len(outs),
        scratch_shapes=list(scratch),
        cost_estimate=cost(us),
        compiler_params=pltpu.CompilerParams(vmem_limit_bytes=vmem),
    )(*args)


def spread_rows():
    same = (iota((SLOTS, EXTRA), 0) // CAP) == iota((SLOTS, EXTRA), 1)
    return same.astype(f32).astype(bf16)


def earlier():
    return (iota((ROWS, ROWS), 0) < iota((ROWS, ROWS), 1)).astype(f32).astype(bf16)


def routing_kernel(routes_t, cot, pick_t, rows_out):
    sub = iota((EXTRA, ROWS), 0)
    mask_t = jnp.zeros((EXTRA, ROWS), f32)
    for k in range(TOP):
        mask_t += (routes_t[k : k + 1, :] == sub).astype(f32)
    mask_tb = mask_t.astype(bf16)
    before_t = nn(mask_tb, earlier())
    slot = iota((CAP, ROWS), 0).astype(f32)
    p_t = jnp.concatenate(
        [
            jnp.where(before_t[e : e + 1] == slot, mask_t[e : e + 1], 0.0).astype(bf16)
            for e in range(OWNERS)
        ],
        axis=0,
    )
    pick_t[...] = p_t
    rows_out[:, :WIDTH] = nn(p_t, cot[...]).astype(bf16)
    rows_out[:, WIDTH:] = nt(p_t, mask_tb).astype(bf16)


def mask_kernel(routes, pick, mask_out):
    lane = iota((ROWS, EXTRA), 1)
    mask = jnp.zeros((ROWS, EXTRA), f32)
    for k in range(TOP):
        mask += (routes[:, k : k + 1] == lane).astype(f32)
    mask_out[...] = mask
    mask_b = mask.astype(bf16)
    before = tn(earlier(), mask_b).astype(bf16)
    spread = spread_rows()
    slot = (iota((ROWS, SLOTS), 1) % CAP).astype(f32)
    pick[...] = jnp.where(nt(before, spread) == slot, nt(mask_b, spread), 0.0).astype(bf16)


def gate_kernel(gate, pick, weights):
    spread = spread_rows()
    high, low = split_two(gate[...])
    w = pick[...].astype(f32) * (nt(high, spread) + nt(low, spread))
    weights[...] = w.astype(bf16)


def swap_halves(t):
    lane = iota(t.shape, 1) % 64
    return jnp.where(lane < 32, pltpu.roll(t, 96, 1), pltpu.roll(t, 32, 1))


def allowed(split, low, rows, keys):
    qi = iota((rows, keys), 0) + low
    kj = iota((rows, keys), 1)
    start = jnp.where(qi >= split, split, 0)
    return (kj <= qi) & (kj >= start)


BLOCK = 256
BLOCKS = GROUP // BLOCK


def head_place(h):
    return h // 2, h % 2, (h // 2) != (h % 2)


def source(z, d):
    return (z + LANES - d) % LANES


def rows_at(start, size, step):
    return pl.ds(pl.multiple_of(start, step), size)


def pack_kernel(
    place, w_query, w_key, w_value, w_router, gains, w_out, own, out_half, *sent
):
    z, core = place[0], place[1]
    select = ((iota((16, EXTRA), 1) - OWNERS) == iota((16, EXTRA), 0)) & (iota((16, EXTRA), 0) < 2)
    small = tn(gains[...], select.astype(f32).astype(bf16)).astype(bf16)
    own[:, 512:640] = small
    own[:, 512 : 512 + OWNERS] = w_router[...]

    def fill(out, dest, rows):
        out[:, :256] = w_query[rows, rows_at(dest * 256, 256, 256)]
        out[:, 256:384] = w_key[rows, rows_at(dest * 128, 128, 128)]
        out[:, 384:512] = w_value[rows, rows_at(dest * 128, 128, 128)]

    fill(own, z, slice(None))
    half = rows_at(core * 128, 128, 128)
    out_half[...] = w_out[half, :]
    for d, out in enumerate(sent):
        fill(out, (z + d + 1) % LANES, half)
        out[:, 512:640] = own[half, 512:640]


def norm_kernel(place, x0, x1, x2, x3, x_ref, factor):
    for d, piece in enumerate((x0, x1, x2, x3)):
        x_ref[rows_at(source(place[0], d) * ROWS, ROWS, 64), :] = piece[...]
    x = x_ref[...].astype(f32)
    r = lax.rsqrt(jnp.mean(x * x, axis=-1, keepdims=True) + epsilon)
    factor[...] = jnp.broadcast_to(r, (GROUP, EXTRA))


def gain_row(small, which):
    select = (iota((16, EXTRA), 1) == OWNERS + which).astype(f32).astype(bf16)
    return nt(select, small)[:1]


def front_kernel(
    split,
    place,
    x_ref,
    factor,
    w_own,
    w_mine,
    w_other,
    cosine,
    sine,
    w_ref,
    normed,
    q_out,
    k_out,
    v_out,
    mixed,
    m0,
    m1,
    m2,
    m3,
):
    z, core = place[0], place[1]
    w_ref[rows_at(z * 256, 256, 256), :] = w_own[...]
    for d in (1, 2, 3):
        start = source(z, d) * 256
        w_ref[rows_at(start + core * 128, 128, 128), :] = w_mine[d - 1]
        w_ref[rows_at(start + (1 - core) * 128, 128, 128), :] = w_other[d - 1]
    x = x_ref[...].astype(f32)
    normed_b = (x * factor[:, :1] * gain_row(w_ref[:, 512:640], 0)).astype(bf16)
    normed[...] = normed_b
    lin = nn(normed_b, w_ref[:, :512])
    c, s = cosine[...], sine[...]
    for g in range(2):
        part = lin[:, 128 * g : 128 * g + 128]
        q_out[:, 128 * g : 128 * g + 128] = (part * c + swap_halves(part) * s).astype(bf16)
    part = lin[:, 256:384]
    key = part * c + swap_halves(part) * s
    key_b = key.astype(bf16)
    k_out[...] = key_b
    value_b = lin[:, 384:512].astype(bf16)
    v_out[...] = value_b
    keys = (key_b, pltpu.roll(key_b.astype(f32), 64, 1).astype(bf16))
    values = (value_b, pltpu.roll(value_b.astype(f32), 64, 1).astype(bf16))
    low_half = iota((BLOCK, 128), 1) < 64
    for i in range(BLOCKS):
        n = (i + 1) * BLOCK
        ok = allowed(split[0], i * BLOCK, BLOCK, n)
        for g in range(2):
            q2 = q_out[i * BLOCK : (i + 1) * BLOCK, 128 * g : 128 * g + 128].astype(f32) * score_scale
            halves = []
            for half in range(2):
                turned = g != half
                mine = low_half if half == 0 else ~low_half
                qh = jnp.where(mine, q2, 0.0).astype(bf16)
                scores = jnp.where(ok, nt(qh, keys[turned][:n]), -1e30)
                top = jnp.max(scores, axis=-1, keepdims=True)
                e = jnp.exp(scores - top)
                share = 1.0 / jnp.sum(e, axis=-1, keepdims=True)
                halves.append(share * nn(e.astype(bf16), values[turned][:n]))
            mixed[i * BLOCK : (i + 1) * BLOCK, 128 * g : 128 * g + 128] = jnp.where(
                low_half, halves[0], halves[1]
            ).astype(bf16)
    for d, out in enumerate((m0, m1, m2, m3)):
        out[...] = mixed[rows_at(((z + d) % LANES) * ROWS, ROWS, 64), :]


def middle_kernel(
    place,
    m0,
    m1,
    m2,
    m3,
    out_own,
    out_mine,
    out_other,
    x_ref,
    router,
    mask,
    pick_t,
    middle,
    second,
    gate,
    rows_out,
    w_out,
    mixed,
):
    z, core = place[0], place[1]
    for d, piece in enumerate((m0, m1, m2, m3)):
        mixed[:, rows_at(source(z, d) * 256, 256, 256)] = piece[...]
    w_out[rows_at(z * 256, 256, 256), :] = out_own[...]
    for d in (1, 2, 3):
        start = source(z, d) * 256
        w_out[rows_at(start + core * 128, 128, 128), :] = out_mine[d - 1]
        w_out[rows_at(start + (1 - core) * 128, 128, 128), :] = out_other[d - 1]
    mid = x_ref[...].astype(f32) + residual_scale * nn(mixed[...], w_out[...])
    middle[...] = mid
    factor = lax.rsqrt(jnp.mean(mid * mid, axis=-1, keepdims=True) + epsilon)
    second_b = (mid * factor * gain_row(router[...], 1)).astype(bf16)
    second[...] = second_b
    chosen = mask[...] > 0.5
    logits = jnp.where(chosen, nn(second_b, router[...]), -1e30)
    top = jnp.max(logits, axis=-1, keepdims=True)
    e = jnp.where(chosen, jnp.exp(logits - top), 0.0)
    gate[...] = e / jnp.sum(e, axis=-1, keepdims=True)
    rows_out[...] = nn(pick_t[...], second_b).astype(bf16)


EXPERT_BLOCK = 512
PARTS = WIDTH // 128
PACKED = PARTS * CAP + 16


def expert_kernel(rows, h_up, w_gate, w_up, *rest):
    g_rows, hidden, g_gate, g_up = rest[-4:]
    r = rows[...]
    gate_lin = nn(r, w_gate[...])
    up_lin = nn(r, w_up[...])
    sig = 1.0 / (1.0 + jnp.exp(-gate_lin))
    act = gate_lin * sig
    hidden_b = (act * up_lin).astype(bf16)
    hidden[...] = hidden_b
    g_hidden = h_up[...].astype(f32)
    g = jnp.sum(hidden_b.astype(f32) * g_hidden, axis=-1, keepdims=True)
    gg = (g_hidden * up_lin * (sig * (1.0 + gate_lin * (1.0 - sig)))).astype(bf16)
    gu = (g_hidden * act).astype(bf16)
    g_gate[...] = gg
    g_up[...] = gu
    result = (nt(gg, w_gate[...]) + nt(gu, w_up[...])).astype(bf16)
    lane, slot = iota((CAP, 128), 1), iota((CAP, 128), 0)
    high = g.astype(bf16).astype(f32)
    for s in range(EXPERT_BLOCK // CAP):
        here = slice(CAP * s, CAP * s + CAP)
        for j in range(PARTS):
            g_rows[s, CAP * j : CAP * j + CAP, :] = result[here, 128 * j : 128 * j + 128]
        spread = jnp.where(
            lane == slot,
            high[here],
            jnp.where(lane == slot + CAP, (g - high)[here], 0.0),
        )
        scalars = jnp.sum(spread, axis=0, keepdims=True)
        g_rows[s, PARTS * CAP :, :] = jnp.broadcast_to(scalars, (16, 128)).astype(bf16)


def row_gate_kernel(me, rows, mask, router, out):
    chosen = mask[...].astype(f32) > 0.5
    logits = jnp.where(chosen, nn(rows[...], router[...]), -1e30)
    top = jnp.max(logits, axis=-1, keepdims=True)
    e = jnp.where(chosen, jnp.exp(logits - top), 0.0)
    total = jnp.sum(e, axis=-1, keepdims=True)
    mine = jnp.sum(jnp.where(iota((SLOTS, EXTRA), 1) == me[0], e, 0.0), axis=-1, keepdims=True)
    out[...] = jnp.broadcast_to(mine / jnp.where(total > 0, total, 1.0), (SLOTS, EXTRA))


def hold_kernel(value, out):
    out[...] = value[...]


def stack_kernel(a, b, c, out):
    out[0], out[1], out[2] = a[...], b[...], c[...]


def expert_call(rows, h_up, w_gate, w_up, after):
    def whole(shape):
        return pl.BlockSpec(shape, lambda i: (0, 0))

    def blocked(width):
        return pl.BlockSpec((EXPERT_BLOCK, width), lambda i: (i, 0))

    return pl.pallas_call(
        expert_kernel,
        name="expert",
        grid=(SLOTS // EXPERT_BLOCK,),
        out_shape=[jax.ShapeDtypeStruct((OWNERS, PACKED, 128), bf16)]
        + [jax.ShapeDtypeStruct((SLOTS, FF), bf16)] * 3,
        in_specs=[blocked(WIDTH), blocked(FF), whole((WIDTH, FF)), whole((WIDTH, FF))]
        + [pl.BlockSpec(memory_space=pltpu.HBM)] * len(after),
        out_specs=[pl.BlockSpec((EXPERT_BLOCK // CAP, PACKED, 128), lambda i: (i, 0, 0))]
        + [blocked(FF)] * 3,
        cost_estimate=cost(15),
        compiler_params=pltpu.CompilerParams(vmem_limit_bytes=60 * 1024 * 1024),
    )(rows, h_up, w_gate, w_up, *after)


def return_kernel(
    place,
    back,
    pick,
    weights,
    middle,
    second,
    gate,
    cot,
    router,
    w_out,
    g_middle_out,
    small_out,
    p0,
    p1,
    p2,
    p3,
    g_branch,
    g_mixed,
):
    lane = iota((ROWS, EXTRA), 1)
    spread = spread_rows()
    scalars = nn(spread[:, :OWNERS], back[:, PARTS * CAP, :])
    offset, lanes = iota((SLOTS, EXTRA), 0) % CAP, iota((SLOTS, EXTRA), 1)
    column = jnp.sum(jnp.where(lanes % CAP == offset, scalars, 0.0), axis=-1, keepdims=True)
    high, low = split_two(spread.astype(f32) * column)
    g_gate = nn(pick[...], high) + nn(pick[...], low)
    probs = gate[...]
    g_logits = probs * (g_gate - jnp.sum(probs * g_gate, axis=-1, keepdims=True))
    high, low = split_two(g_logits)
    w = router[...]
    pieces = [
        back[:, CAP * j : CAP * j + CAP, :].reshape(SLOTS, 128) for j in range(PARTS)
    ]
    summed = [
        nn(weights[...], jnp.concatenate(pieces[j : j + 2], axis=1)) for j in range(0, PARTS, 2)
    ]
    g_second = jnp.concatenate(summed, axis=1) + (nt(high, w) + nt(low, w))
    mid = middle[...]
    factor = lax.rsqrt(jnp.mean(mid * mid, axis=-1, keepdims=True) + epsilon)
    z = mid * factor
    t = g_second * gain_row(w, 1)
    g_middle = cot[...].astype(f32) + factor * (t - z * jnp.mean(t * z, axis=-1, keepdims=True))
    g_middle_out[...] = g_middle
    branch_b = (residual_scale * g_middle).astype(bf16)
    g_branch[...] = branch_b
    g_mixed[...] = nt(branch_b, w_out[...]).astype(bf16)
    for d, out in enumerate((p0, p1, p2, p3)):
        there = rows_at(((place[0] + d) % LANES) * 256, 256, 256)
        out[:, :256] = g_mixed[:, there]
        out[:, 256:] = g_branch[:, there]
    s = second[...]
    one = (lane == OWNERS).astype(f32).astype(bf16)
    ph, plow = split_two(g_second * z)
    small_out[...] = tn(s, high) + tn(s, low) + tn(ph, one) + tn(plow, one)


def back_kernel(
    split,
    place,
    p0,
    p1,
    p2,
    p3,
    m0,
    m1,
    m2,
    m3,
    q_ref,
    k_ref,
    v_ref,
    normed,
    x_ref,
    w_ref,
    cosine,
    sine,
    small_in,
    keep,
    give,
    n0,
    n1,
    n2,
    n3,
    grads,
    g_normed_out,
    g_mixed,
    g_branch,
    g_query,
    g_key,
    g_value,
):
    z, core = place[0], place[1]
    for d, piece in enumerate((p0, p1, p2, p3)):
        rows = rows_at(source(z, d) * ROWS, ROWS, 64)
        g_mixed[rows, :] = piece[:, :256]
        g_branch[rows, :] = piece[:, 256:]
    key_b, value_b = k_ref[...], v_ref[...]
    keys = (key_b, pltpu.roll(key_b.astype(f32), 64, 1).astype(bf16))
    values = (value_b, pltpu.roll(value_b.astype(f32), 64, 1).astype(bf16))
    g_key[...] = jnp.zeros_like(g_key)
    g_value[...] = jnp.zeros_like(g_value)
    low_half = iota((BLOCK, 128), 1) < 64
    for i in range(BLOCKS):
        n = (i + 1) * BLOCK
        here = slice(i * BLOCK, (i + 1) * BLOCK)
        ok = allowed(split[0], i * BLOCK, BLOCK, n)
        for g in range(2):
            q2 = q_ref[here, 128 * g : 128 * g + 128].astype(f32) * score_scale
            gm2 = g_mixed[here, 128 * g : 128 * g + 128].astype(f32)
            halves = []
            for half in range(2):
                turned = int(g != half)
                mine = low_half if half == 0 else ~low_half
                qh = jnp.where(mine, q2, 0.0).astype(bf16)
                gm = jnp.where(mine, gm2, 0.0).astype(bf16)
                scores = jnp.where(ok, nt(qh, keys[turned][:n]), -1e30)
                top = jnp.max(scores, axis=-1, keepdims=True)
                e = jnp.exp(scores - top)
                share = 1.0 / jnp.sum(e, axis=-1, keepdims=True)
                gp = nt(gm, values[turned][:n])
                mean = share * jnp.sum(e * gp, axis=-1, keepdims=True)
                gs = (e * (gp - mean)).astype(bf16)
                halves.append(share * nn(gs, keys[turned][:n]))
                g_key[turned, :n, :] += tn(gs, (share * qh.astype(f32)).astype(bf16))
                g_value[turned, :n, :] += tn(e.astype(bf16), (share * gm.astype(f32)).astype(bf16))
            g_query[here, 128 * g : 128 * g + 128] = score_scale * jnp.where(
                low_half, halves[0], halves[1]
            )
    c, s = cosine[...], sine[...]

    def unturn(t):
        return (t * c - swap_halves(t) * s).astype(bf16)

    g_lin = jnp.concatenate(
        [
            unturn(g_query[:, :128]),
            unturn(g_query[:, 128:]),
            unturn(g_key[0] + pltpu.roll(g_key[1], 64, 1)),
            (g_value[0] + pltpu.roll(g_value[1], 64, 1)).astype(bf16),
        ],
        axis=1,
    )
    grads[:, :512] = tn(normed[...], g_lin).astype(bf16)
    for d, piece in enumerate((m0, m1, m2, m3)):
        grads[rows_at(source(z, d) * 256, 256, 256), 512:768] = tn(piece[...], g_branch[...]).astype(bf16)
    g_normed = nt(g_lin, w_ref[:, :512])
    g_normed_out[...] = g_normed.astype(bf16)
    x = x_ref[...].astype(f32)
    y = x * lax.rsqrt(jnp.mean(x * x, axis=-1, keepdims=True) + epsilon)
    one = (iota((GROUP, EXTRA), 1) == OWNERS + 1).astype(f32).astype(bf16)
    ph, plow = split_two(g_normed * y)
    grads[:, 768:] = (small_in[...] + tn(ph, one) + tn(plow, one)).astype(bf16)
    for a in range(LANES):
        keep[128 * a : 128 * a + 128, :] = grads[rows_at(a * 256 + core * 128, 128, 128), :]
        give[128 * a : 128 * a + 128, :] = grads[rows_at(a * 256 + (1 - core) * 128, 128, 128), :]
    for d, out in enumerate((n0, n1, n2, n3)):
        out[...] = g_normed_out[rows_at(((z + d) % LANES) * ROWS, ROWS, 64), :]


def input_kernel(n0, n1, n2, n3, x_ref, g_middle, small, out):
    g = n0[...].astype(f32) + n1[...].astype(f32) + n2[...].astype(f32) + n3[...].astype(f32)
    x = x_ref[...].astype(f32)
    factor = lax.rsqrt(jnp.mean(x * x, axis=-1, keepdims=True) + epsilon)
    y = x * factor
    t = g * gain_row(small[...], 0)
    out[...] = g_middle[...] + factor * (t - y * jnp.mean(t * y, axis=-1, keepdims=True))


def add_kernel(a, b, out):
    out[...] = (a[...].astype(f32) + b[...].astype(f32)).astype(bf16)


def strip_kernel(arrived, out):
    total = jnp.sum(arrived[...].astype(f32).reshape(LANES, 16, 8, 768 + EXTRA), axis=1)
    parts = [total[a, :, :256] for a in range(LANES)]
    parts += [total[a, :, 256:384] for a in range(LANES)]
    parts += [total[a, :, 384:512] for a in range(LANES)]
    parts += [total[a, :, 512:768] for a in range(LANES)]
    strip = jnp.concatenate(parts + [jnp.sum(total[:, :, 768:], axis=0)], axis=1)
    out[...] = jnp.concatenate([strip] * 16, axis=0).astype(bf16)


def final_kernel(place, piece, *refs):
    query, key, value, out, router, gain_m, gain_a = refs[-7:]
    query[...] = piece[:, :1024].astype(f32)
    key[...] = piece[:, 1024:1536].astype(f32)
    value[...] = piece[:, 1536:2048].astype(f32)
    out[...] = piece[:, 2048:3072].astype(f32)
    select = iota((64, EXTRA), 1) == iota((64, EXTRA), 0)
    small = nt(select.astype(f32).astype(bf16), piece[:, 3072:])
    router[...] = small[:OWNERS]
    gain_m[...] = small[OWNERS : OWNERS + 1]
    gain_a[...] = small[OWNERS + 1 : OWNERS + 2]


def final_call(half, place, piece, before):
    def rows(width):
        return pl.BlockSpec((128, width), lambda i, p: ((p[1] + half) % 2, 0))

    def columns(height):
        return pl.BlockSpec((height, 128), lambda i, p: (0, (p[1] + half) % 2))

    widths, heights = (1024, 512, 512, 1024), (OWNERS, 1, 1)
    shapes = [(256, w) for w in widths] + [(h, 256) for h in heights]
    return pl.pallas_call(
        final_kernel,
        name="final",
        out_shape=[jax.ShapeDtypeStruct(s, f32) for s in shapes],
        grid_spec=pltpu.PrefetchScalarGridSpec(
            num_scalar_prefetch=1,
            grid=(1,),
            in_specs=[pl.BlockSpec((128, 3072 + EXTRA), lambda i, p: (0, 0))]
            + [pl.BlockSpec(memory_space=pltpu.HBM)] * len(before),
            out_specs=[rows(w) for w in widths] + [columns(h) for h in heights],
        ),
        input_output_aliases={2 + i: i for i in range(len(before))},
        cost_estimate=cost(1),
        compiler_params=pltpu.CompilerParams(vmem_limit_bytes=VMEM),
    )(place, piece, *before)


def z_shift(value, d):
    return lax.ppermute(value, "wshard", [(i, (i + d) % LANES) for i in range(LANES)])


def z_shifts(values):
    return [z_shift(v, d) for d, v in zip((1, 2, 3), values)]


def other_core(value):
    return lax.ppermute(value, "expert", [(i, i ^ 1) for i in range(OWNERS)])


def to_owners(value):
    return lax.all_to_all(value, "expert", 0, 0, tiled=True)


def local(
    tokens,
    w_query,
    w_key,
    w_value,
    w_out,
    w_router,
    gain_attn,
    gain_moe,
    w_gate,
    w_up,
    w_down,
    routes,
    seq_split,
    cotangent,
):
    z = lax.axis_index("wshard")
    me = lax.axis_index("expert")
    core = me % 2
    place = jnp.stack([z, core]).astype(jnp.int32)
    w_gate, w_up, w_down = w_gate[0], w_up[0], w_down[0]

    routes_t = routes.T
    pick_t, ups_send = call(
        routing_kernel,
        "routing",
        [((SLOTS, ROWS), bf16), ((SLOTS, WIDTH + EXTRA), bf16)],
        (routes_t, cotangent),
        4,
        vmem=ALL_VMEM,
    )
    ups = to_owners(ups_send.reshape(OWNERS, CAP, WIDTH + EXTRA)).reshape(SLOTS, WIDTH + EXTRA)
    pick, mask = call(
        mask_kernel, "mask", [((ROWS, SLOTS), bf16), ((ROWS, EXTRA), f32)], (routes,), 3
    )

    split_at = seq_split[0]
    places = jnp.arange(GROUP, dtype=jnp.int32)
    position = jnp.where(places >= split_at, places - split_at, places).astype(f32)
    exponent = jnp.arange(32, dtype=f32) * (2.0 / 64)
    angles = position[:, None] * jnp.power(rope_base, -exponent)[None, :]
    cosine, sine = jnp.cos(angles), jnp.sin(angles)
    cosine = jnp.concatenate([cosine] * 4, axis=1)
    sine = jnp.concatenate([-sine, sine] * 2, axis=1)

    gains = jnp.pad(jnp.stack([gain_attn, gain_moe]), ((0, 14), (0, 0)))
    w_own, out_half, *w_sent = call(
        pack_kernel,
        "pack",
        [((256, 640), bf16), ((128, WIDTH), bf16)] + [((128, 640), bf16)] * 3,
        (place, w_query, w_key, w_value, w_router, gains, w_out),
        1,
        smem=1,
        after=(pick_t,),
    )
    w_pieces = z_shifts(w_sent)
    w_mine = call(
        stack_kernel, "stack", [((3, 128, 640), bf16)], w_pieces, 1, after=(cosine, sine)
    )[0]
    w_other = other_core(w_mine)
    tokens_held = call(
        hold_kernel, "hold", [((ROWS, WIDTH), bf16)], (tokens,), 1, after=(w_pieces[0],)
    )[0]
    x_pieces = [tokens] + z_shifts([tokens_held] * 3)
    out_halves = z_shifts([out_half] * 3)
    x_all, factor_all = call(
        norm_kernel,
        "norm",
        [((GROUP, WIDTH), bf16), ((GROUP, EXTRA), f32)],
        (place, *x_pieces),
        2,
        smem=1,
    )

    w_all, normed, query, key, value, mixed, *mixed_sent = call(
        front_kernel,
        "attention",
        [
            ((WIDTH, 640), bf16),
            ((GROUP, WIDTH), bf16),
            ((GROUP, 256), bf16),
            ((GROUP, 128), bf16),
            ((GROUP, 128), bf16),
            ((GROUP, 256), bf16),
        ]
        + [((ROWS, 256), bf16)] * 4,
        (seq_split, place, x_all, factor_all, w_own, w_mine, w_other, cosine, sine),
        8,
        smem=2,
    )
    small_all = w_all[:, 512:]
    out_mine = call(
        stack_kernel, "stack", [((3, 128, WIDTH), bf16)], out_halves, 1, after=(mixed,)
    )[0]
    out_other = other_core(out_mine)
    middle, second, gate, rows_send, out_all = call(
        middle_kernel,
        "middle",
        [
            ((ROWS, WIDTH), f32),
            ((ROWS, WIDTH), bf16),
            ((ROWS, EXTRA), f32),
            ((SLOTS, WIDTH), bf16),
            ((WIDTH, WIDTH), bf16),
        ],
        (
            place,
            mixed_sent[0],
            *z_shifts(mixed_sent[1:]),
            w_out,
            out_mine,
            out_other,
            tokens,
            small_all,
            mask,
            pick_t,
        ),
        6,
        vmem=ALL_VMEM,
        smem=1,
        scratch=[pltpu.VMEM((ROWS, WIDTH), bf16)],
    )
    rows_in = to_owners(rows_send.reshape(OWNERS, CAP, WIDTH)).reshape(SLOTS, WIDTH)
    mixed_pieces = [mixed] + z_shifts([mixed] * 3)

    weights = call(gate_kernel, "gates", [((ROWS, SLOTS), bf16)], (gate, pick), 1)[0]

    up_rows = ups[:, :WIDTH]
    h_up = (residual_scale * nt(up_rows, w_down)).astype(bf16)
    g_rows, hidden, g_gate, g_up = expert_call(rows_in, h_up, w_gate, w_up, mixed_pieces)
    back = to_owners(g_rows)

    row_gate = call(
        row_gate_kernel,
        "row_gates",
        [((SLOTS, EXTRA), f32)],
        (me.reshape(1), rows_in, ups[:, WIDTH:], small_all),
        4,
        smem=1,
        after=(hidden,),
    )[0][:, :1]
    g_out = (residual_scale * row_gate * up_rows.astype(f32)).astype(bf16)
    gate_grad = tn(rows_in, (row_gate * g_gate.astype(f32)).astype(bf16)).astype(bf16)
    up_grad = tn(rows_in, (row_gate * g_up.astype(f32)).astype(bf16)).astype(bf16)
    down_grad = tn(hidden, g_out).astype(bf16)

    def shared_sum(grad):
        parts = grad.reshape(LANES, -1, grad.shape[1])

        def part(d):
            return lax.dynamic_index_in_dim(parts, (z + d) % LANES, 0, keepdims=False)

        total = part(0).astype(f32)
        for piece in z_shifts([part(d) for d in (1, 2, 3)]):
            total += piece.astype(f32)
        return total

    gate_share, up_share, down_share = (shared_sum(g) for g in (gate_grad, up_grad, down_grad))
    expert_out = nn(hidden, w_down).astype(bf16)
    out_back = to_owners(expert_out.reshape(OWNERS, CAP, WIDTH))

    g_middle, small_grad, *branch_sent = call(
        return_kernel,
        "return",
        [((ROWS, WIDTH), f32), ((WIDTH, EXTRA), f32)] + [((ROWS, 512), bf16)] * 4,
        (place, back, pick, weights, middle, second, gate, cotangent, small_all, out_all),
        7,
        smem=1,
        scratch=[pltpu.VMEM((ROWS, WIDTH), bf16), pltpu.VMEM((ROWS, WIDTH), bf16)],
        after=(gate_share, up_share, down_share),
    )
    wide = 768 + EXTRA
    keep, give, *normed_sent = call(
        back_kernel,
        "attention_back",
        [((512, wide), bf16)] * 2 + [((ROWS, WIDTH), bf16)] * 4,
        (
            seq_split,
            place,
            branch_sent[0],
            *z_shifts(branch_sent[1:]),
            *mixed_pieces,
            query,
            key,
            value,
            normed,
            x_all,
            w_all,
            cosine,
            sine,
            small_grad,
        ),
        18,
        vmem=ALL_VMEM,
        smem=2,
        scratch=[
            pltpu.VMEM((WIDTH, wide), bf16),
            pltpu.VMEM((GROUP, WIDTH), bf16),
            pltpu.VMEM((GROUP, 256), bf16),
            pltpu.VMEM((GROUP, 256), bf16),
            pltpu.VMEM((GROUP, 256), f32),
            pltpu.VMEM((2, GROUP, 128), f32),
            pltpu.VMEM((2, GROUP, 128), f32),
        ],
    )

    output = middle + residual_scale * nn(weights, out_back.reshape(SLOTS, WIDTH))

    input_grad = call(
        input_kernel,
        "input_grad",
        [((ROWS, WIDTH), f32)],
        (normed_sent[0], *z_shifts(normed_sent[1:]), tokens, g_middle, small_all),
        7,
    )[0]

    chip = call(
        add_kernel, "add", [((512, wide), bf16)], (keep, other_core(give)), 1, after=(out_back,)
    )[0]
    groups = [
        [(2 * xy + c) * LANES + a for a in range(LANES) for xy in range(OWNERS // 2)]
        for c in range(2)
    ]
    arrived = lax.all_to_all(
        chip.reshape(64, 8, wide),
        ("expert", "wshard"),
        0,
        0,
        tiled=True,
        axis_index_groups=groups,
    )
    strips = call(
        strip_kernel,
        "strip",
        [((128, 3072 + EXTRA), bf16)],
        (arrived.reshape(512, wide),),
        2,
        after=(output, input_grad),
    )[0]
    shared = lax.all_to_all(
        strips.reshape(OWNERS // 2, 8, 3072 + EXTRA),
        "expert",
        0,
        0,
        tiled=True,
        axis_index_groups=[[2 * xy + c for xy in range(OWNERS // 2)] for c in range(2)],
    ).reshape(128, 3072 + EXTRA)
    dense = final_call(0, place, shared, ())
    dense = final_call(1, place, other_core(shared), dense)
    grad_query, grad_key, grad_value, grad_out, grad_router, grad_gain_m, grad_gain_a = dense

    return (
        output,
        input_grad,
        grad_query,
        grad_key,
        grad_value,
        grad_out,
        grad_router.T,
        grad_gain_a[0],
        grad_gain_m[0],
        gate_share[None],
        up_share[None],
        down_share[None],
    )


def solution(mesh):
    rows = P(("expert", "wshard"), None)
    dense = P("wshard", None)
    expert = P("expert", None, None)
    shard = P("expert", "wshard", None)
    in_specs = (rows,) + (dense,) * 5 + (P("wshard"),) * 2 + (expert,) * 3
    in_specs += (rows, P("expert"), rows)
    out_specs = (rows, rows) + (dense,) * 5 + (P("wshard"),) * 2 + (shard,) * 3
    return jax.shard_map(local, mesh=mesh, in_specs=in_specs, out_specs=out_specs, check_vma=False)
```
